128 devices in a mesh: lon: 32 (over z, y, core), lat: 4 (over x).
Axes of the slice: x: 4, y: 4, z: 4, core: 2. Of those that a mesh axis runs over, the one named last changes fastest.
Arguments:
- state: float32 [32, 2048, 6, 128], P('lat', 'lon'), may hold values from -4 to 4
- background: float32 [32, 2048, 6, 128], P('lat', 'lon'), may hold values from -4 to 4
- diffusivity: float32 [32, 2048, 128], P('lat', 'lon'), may hold values from 0.03 to 0.2
- radiances: bfloat16 [2, 32, 2048, 512], P(None, 'lat', 'lon'), may hold values from -5 to 5
- owners: int32 [2, 4, 512], P(None, 'lat', 'lon'), may hold values from 0 to 31, as said below
- first_layer: bfloat16 [32, 768, 1024], P('lon'), may hold values from -0.21875 to 0.21875
- second_layer: bfloat16 [32, 1024, 1024], P('lon'), may hold values from -0.1875 to 0.1875
- third_layer: bfloat16 [32, 1024, 512], P('lon'), may hold values from -0.1875 to 0.1875
- channel_weight: float32 [32, 512], P('lon'), may hold values from 0.3 to 3
Outputs:
- gradient: float32 [32, 2048, 6, 128], P('lat', 'lon')
The draws below stay inside these ranges and needn't reach their ends.
Inputs may be any that keep to these rules, and one draw needn't show every extreme that they name: `owners`: every block is observed by one instrument in every slot. In each slot a device sends at most 1 of its blocks to one instrument, and an instrument receives at most 24 blocks from the devices of one latitude index; both bounds are reached in every slot and latitude index.
All inputs are finite; a program needn't handle non-finite values.
Results may differ from the reference program's by a relative error of at most 0.0024.
Values may be sent and summed in bfloat16 or wider, within the bound.
A program may use at most 128 MiB of HBM per device.

```python
import math
import jax
import jax.numpy as jnp
from jax import lax

F = 6
LEV = 128
CIN = 768
H1 = 1024
H2 = 1024
CH = 512
CLAT = 8
CLON = 64
SLOTS = 2
BLK = 32
NB = 16
INSTR = 32
NLAT = 32
NLON = 2048
N_LON = 32
N_LAT = 4


def draw_owners(key, part):
    stride = N_LON // NB
    extra = NB // 2
    row_keys = jax.random.split(jax.random.fold_in(key, 7), SLOTS * N_LAT)

    def one_row(row_key):
        key_relabel, key_offset, key_hot, key_score, key_order = jax.random.split(row_key, 5)
        relabel = jax.random.permutation(key_relabel, N_LON).astype(jnp.int32)
        offset = jax.random.permutation(key_offset, N_LON).astype(jnp.int32)
        hottest = jax.random.randint(key_hot, (), 0, N_LON, dtype=jnp.int32)
        block_steps = jnp.arange(NB, dtype=jnp.int32) * stride
        target = (offset[:, None] + block_steps[None, :]) % N_LON
        apart = (hottest - offset) % stride != 0
        eligible = (offset != hottest) & (apart | (stride == 1))
        score = jax.random.permutation(key_score, N_LON).astype(jnp.int32) + jnp.where(eligible, N_LON, 0)
        standing = jnp.sum(score[None, :] > score[:, None], axis=1)
        chosen = standing < extra
        target = target.at[:, 0].set(jnp.where(chosen, hottest, target[:, 0]))
        owner_ids = relabel[target]
        order_keys = jax.random.split(key_order, N_LON)
        shuffles = jax.vmap(lambda shuffle_key: jax.random.permutation(shuffle_key, NB))(order_keys)
        mixed = jnp.take_along_axis(owner_ids, shuffles.astype(jnp.int32), axis=1)
        return mixed.reshape(N_LON * NB).astype(jnp.int32)
    owner_rows = jax.vmap(one_row)(row_keys)
    return owner_rows.reshape(SLOTS, N_LAT, N_LON * NB)


def shard_levels(rng, extent, shards, low, top_value):
    gain = 1.0
    for axis_at, blocks in shards:
        draws = jax.random.uniform(jax.random.fold_in(jax.random.fold_in(rng, 6), axis_at), (blocks,), jnp.float32, low / len(shards), top_value / len(shards))
        gain = gain * jnp.repeat(jnp.exp(draws), extent[axis_at] // blocks).reshape((-1,) + (1,) * (len(extent) - 1 - axis_at))
    return gain


def centred(rng, shape, deviation, bound, cuts=(), held_as=jnp.bfloat16):
    result = deviation * jax.random.normal(rng, shape, jnp.float32)
    if cuts:
        result = result * shard_levels(rng, shape, cuts, -0.22, 0.18)
    return jnp.clip(result, -bound, bound).astype(held_as)


def setup_inputs(seed: int = 0) -> dict:
    key_list = jax.random.split(jax.random.key(seed), 10)
    state = centred(key_list[0], (NLAT, NLON, F, LEV), 1.0, 4.0, ((0, 4), (1, 32)), jnp.float32)
    background = centred(key_list[1], (NLAT, NLON, F, LEV), 1.0, 4.0, ((0, 4), (1, 32)), jnp.float32)
    diffusivity = jnp.clip(jnp.exp(math.log(0.2) - 1.89712 * jax.random.uniform(key_list[2], (NLAT, NLON, LEV), jnp.float32) ** shard_levels(key_list[2], (NLAT, NLON, LEV), ((0, 4), (1, 32)), -0.2, 0.2)), 0.03, 0.2)
    radiances = centred(key_list[3], (SLOTS, NLAT, NLON, CH), 1.0, 5.0, ((1, 4), (2, 32)))
    owners = draw_owners(jax.random.fold_in(key_list[9], 71), 0)
    first_layer = centred(key_list[5], (INSTR, CIN, H1), CIN ** -0.5, 0.21875, ((0, 32),))
    second_layer = centred(key_list[6], (INSTR, H1, H2), H1 ** -0.5, 0.1875, ((0, 32),))
    third_layer = centred(key_list[7], (INSTR, H2, CH), H2 ** -0.5, 0.1875, ((0, 32),))
    channel_weight = jnp.clip(jnp.exp(math.log(3.0) - 2.3025851 * jax.random.uniform(key_list[8], (INSTR, CH), jnp.float32) ** shard_levels(key_list[8], (INSTR, CH), ((0, 32),), -0.2, 0.2)), 0.3, 3.0)
    return {"state": state, "background": background, "diffusivity": diffusivity, "radiances": radiances, "owners": owners, "first_layer": first_layer, "second_layer": second_layer, "third_layer": third_layer, "channel_weight": channel_weight}


ADVECTION = 0.25
VERTICAL = 0.1

def stencil(padded, kappa):
    centre = padded[1:-1, 1:-1]
    northern = padded[2:, 1:-1]
    southern = padded[:-2, 1:-1]
    eastern = padded[1:-1, 2:]
    western = padded[1:-1, :-2]
    zonal_wind = centre[:, :, 0:1]
    meridional = centre[:, :, 1:2]
    transport = 0.5 * ADVECTION * (zonal_wind * (eastern - western) + meridional * (northern - southern))
    spread = eastern + western + northern + southern - 4.0 * centre
    zero_level = jnp.zeros_like(centre[..., :1])
    upper_level = jnp.concatenate([centre[..., 1:], zero_level], axis=-1)
    lower_level = jnp.concatenate([zero_level, centre[..., :-1]], axis=-1)
    return centre - transport + kappa[:, :, None, :] * spread + VERTICAL * (upper_level + lower_level - 2.0 * centre)

def advance(field, kappa):
    padded = jnp.pad(field, ((1, 1), (0, 0), (0, 0), (0, 0)))
    padded = jnp.concatenate([padded[:, -1:], padded, padded[:, :1]], axis=1)
    return stencil(padded, kappa)

def slope(values):
    sigma = jax.nn.sigmoid(values)
    return sigma * (1.0 + values * (1.0 - sigma))

def radiance_gradient(columns, targets, active, first_matrix, second_matrix, third_matrix, channel_scale):
    pre_one = jnp.dot(columns, first_matrix, preferred_element_type=jnp.float32)
    act_one = jax.nn.silu(pre_one).astype(jnp.bfloat16)
    pre_two = jnp.dot(act_one, second_matrix, preferred_element_type=jnp.float32)
    act_two = jax.nn.silu(pre_two).astype(jnp.bfloat16)
    evolved = jnp.dot(act_two, third_matrix, preferred_element_type=jnp.float32)
    misfit = (active[:, None] * channel_scale[None, :] * (evolved - targets.astype(jnp.float32))).astype(jnp.bfloat16)
    back_two = jnp.dot(misfit, third_matrix.T, preferred_element_type=jnp.float32)
    grad_two = (back_two * slope(pre_two)).astype(jnp.bfloat16)
    back_one = jnp.dot(grad_two, second_matrix.T, preferred_element_type=jnp.float32)
    grad_one = (back_one * slope(pre_one)).astype(jnp.bfloat16)
    return jnp.dot(grad_one, first_matrix.T, preferred_element_type=jnp.float32).astype(jnp.bfloat16)

def forcing(field, targets, owner_slot, first_layer, second_layer, third_layer, channel_weight):
    width_in = F * LEV
    channels = targets.shape[-1]
    column_blocks = field.astype(jnp.bfloat16).reshape(N_LAT, CLAT, N_LON, CLON, width_in).transpose(0, 2, 1, 3, 4).reshape(-1, BLK, width_in)
    target_blocks = targets.reshape(N_LAT, CLAT, N_LON, CLON, channels).transpose(0, 2, 1, 3, 4).reshape(-1, BLK, channels)
    owner_flat = owner_slot.reshape(-1).astype(jnp.int32)

    def one_block(item):
        block_columns, block_targets, owner_id = item
        return radiance_gradient(block_columns, block_targets, jnp.ones((BLK,), jnp.float32), first_layer[owner_id], second_layer[owner_id], third_layer[owner_id], channel_weight[owner_id])
    grads = lax.map(one_block, (column_blocks, target_blocks, owner_flat))
    grads = grads.reshape(N_LAT, N_LON, CLAT, CLON, width_in).transpose(0, 2, 1, 3, 4).reshape(NLAT, NLON, F, LEV)
    return grads.astype(jnp.float32)

def reference(state, background, diffusivity, radiances, owners, first_layer, second_layer, third_layer, channel_weight):
    first_state = advance(state, diffusivity)
    second_state = advance(first_state, diffusivity)
    forcing_one = forcing(first_state, radiances[0], owners[0], first_layer, second_layer, third_layer, channel_weight)
    forcing_two = forcing(second_state, radiances[1], owners[1], first_layer, second_layer, third_layer, channel_weight)
    _, pull_one = jax.vjp(lambda field: advance(field, diffusivity), first_state)
    costate = forcing_one + pull_one(forcing_two)[0]
    _, pull_zero = jax.vjp(lambda field: advance(field, diffusivity), state)
    return state - background + pull_zero(costate)[0]
```

```python
import functools

import jax
import jax.numpy as jnp
from jax import lax
from jax.experimental import pallas as pl
from jax.experimental.pallas import tpu as pltpu
from jax.sharding import PartitionSpec as P

MESH = pl.DeviceIdType.MESH
F32 = jnp.float32
BF16 = jnp.bfloat16
ADVECT = 0.125
VERTICAL = 0.1
BLK = 32
CHUNK = 8
TILE = 256
PAD = 8


def torus(n_lon):
    chips = n_lon // 2
    ny = 1
    while ny * ny < chips:
        ny *= 2
    return chips // ny, ny


def offset_order(n_lon):
    nz, ny = torus(n_lon)

    def hops(d):
        return min(d[0], nz - d[0]) + min(d[1], ny - d[1])

    chips = []
    for d in sorted(((a, b) for a in range(nz) for b in range(ny) if a or b), key=lambda d: (hops(d), d)):
        opposite = ((nz - d[0]) % nz, (ny - d[1]) % ny)
        for e in (d, opposite):
            if e not in chips:
                chips.append(e)
    return [(0, 0, 0), (0, 0, 1)] + [(a, b, c) for c in (0, 1) for a, b in chips]


def kernel(
    n_lon, n_lat, pick, slotk,
    st, bg, kd, rad, w1h, w2h, w3h, cwh,
    out,
    s0, s1, kap, rst, cols, send_r, send_c, recv_r, recv_c, rep_s, rep_0, rep_1,
    w1, w2, w3, cw, bgv, frc, acc, north, south, flux, edge_s, edge_r,
    a1, g1, a2, g2, mis, gg2, gg1,
    load_sem, out_sem, cs_sem, cr_sem, rs_sem, rr_sem, ps_sem, pr_sem,
    ns_s, ns_r, ew_s, ew_r,
):
    rows, fields, width, levels = st.shape
    halves = width // BLK
    nz, ny = torus(n_lon)
    order = offset_order(n_lon)
    chunk = min(CHUNK, n_lon // 4)
    chunks = n_lon // chunk
    lon = lax.axis_index("lon")
    lat = lax.axis_index("lat")
    core = lax.rem(lon, 2)
    yy = lax.rem(lon // 2, ny)
    zz = lon // (2 * ny)
    z_at = [lax.rem(zz + d, nz) * (2 * ny) for d in range(nz)]
    y_at = [lax.rem(yy + d, ny) * 2 for d in range(ny)]
    c_at = [core, 1 - core]

    rep_r = (rep_0, rep_1)

    def to(k):
        a, b, c = order[k]
        return (z_at[a] + y_at[b] + c_at[c], lat)

    def back(k):
        a, b, c = order[k]
        return (z_at[(nz - a) % nz] + y_at[(ny - b) % ny] + c_at[c], lat)

    up = (lon, lax.rem(lat + 1, n_lat))
    down = (lon, lax.rem(lat + n_lat - 1, n_lat))
    east = (lax.rem(lon + 1, n_lon), lat)
    west = (lax.rem(lon + n_lon - 1, n_lon), lat)
    inner = pl.ds(PAD, width)

    loads = [
        (st, s0.at[pl.ds(1, rows), :, inner, :]),
        (kd, kap), (rad, rst), (w1h, w1), (w2h, w2), (w3h, w3), (cwh, cw), (bg, bgv),
    ]
    loads = [pltpu.make_async_copy(src, dst, load_sem.at[i]) for i, (src, dst) in enumerate(loads)]
    for load in loads:
        load.start()

    barrier = pltpu.get_barrier_semaphore()
    for k in range(1, n_lon):
        pl.semaphore_signal(barrier, inc=1, device_id=to(k), device_id_type=MESH)
    for there in (up, down):
        pl.semaphore_signal(barrier, inc=1, device_id=there, device_id_type=MESH)
    pl.semaphore_wait(barrier, n_lon + 1)

    def remote(src, dst, send_sem, recv_sem, there):
        return pltpu.make_async_remote_copy(
            src_ref=src, dst_ref=dst, send_sem=send_sem, recv_sem=recv_sem,
            device_id=there, device_id_type=MESH,
        )

    def send_rows(phase, row_up, to_up, row_down, to_down):
        remote(row_up, to_up, ns_s.at[phase, 0], ns_r.at[phase, 0], up).start()
        remote(row_down, to_down, ns_s.at[phase, 1], ns_r.at[phase, 1], down).start()

    def send_edges(phase):
        for side, there in ((0, east), (1, west)):
            remote(
                edge_s.at[phase, side], edge_r.at[phase, side],
                ew_s.at[phase, side], ew_r.at[phase, side], there,
            ).start()

    def wait_halo(phase, row_up, to_up, row_down, to_down):
        remote(row_up, to_up, ns_s.at[phase, 0], ns_r.at[phase, 0], up).wait()
        remote(row_down, to_down, ns_s.at[phase, 1], ns_r.at[phase, 1], down).wait()
        for side, there in ((0, east), (1, west)):
            remote(
                edge_s.at[phase, side], edge_r.at[phase, side],
                ew_s.at[phase, side], ew_r.at[phase, side], there,
            ).wait()

    def state_rows(s):
        return (
            s.at[rows, :, inner, :], s.at[0, :, inner, :],
            s.at[1, :, inner, :], s.at[rows + 1, :, inner, :],
        )

    def send_state(phase, s):
        send_rows(phase, *state_rows(s))

        @pl.loop(0, rows)
        def _(i):
            for f in range(fields):
                edge_s[phase, 0, i, f : f + 1, :] = s[i + 1, f, PAD + width - 1 : PAD + width, :]
                edge_s[phase, 1, i, f : f + 1, :] = s[i + 1, f, PAD : PAD + 1, :]

        send_edges(phase)

    def take_state(phase, s):
        wait_halo(phase, *state_rows(s))

        @pl.loop(0, rows)
        def _(i):
            for f in range(fields):
                s[i + 1, f, PAD - 1 : PAD, :] = edge_r[phase, 0, i, f : f + 1, :]
                s[i + 1, f, PAD + width : PAD + width + 1, :] = edge_r[phase, 1, i, f : f + 1, :]

        @pl.when(lat == 0)
        def _():
            s[0, :, PAD : PAD + width, :] = jnp.zeros((fields, width, levels), F32)

        @pl.when(lat == n_lat - 1)
        def _():
            s[rows + 1, :, PAD : PAD + width, :] = jnp.zeros((fields, width, levels), F32)

    level = lax.broadcasted_iota(jnp.int32, (BLK, levels), 1)
    from_below = jnp.where(level == 0, 0.0, VERTICAL).astype(F32)
    from_above = jnp.where(level == levels - 1, 0.0, VERTICAL).astype(F32)

    def vertical(v):
        return from_below * pltpu.roll(v, 1, 1) + from_above * pltpu.roll(v, levels - 1, 1)

    def advance(s, slot, keep):
        @pl.loop(0, rows)
        def _(i):
            for h in range(halves):
                at = PAD + h * BLK
                k = kap[i, h * BLK : (h + 1) * BLK, :]
                u = ADVECT * s[i + 1, 0, at : at + BLK, :]
                v = ADVECT * s[i + 1, 1, at : at + BLK, :]
                k_e, k_w, k_n, k_s = k - u, k + u, k - v, k + v
                k_c = (1.0 - 2.0 * VERTICAL) - 4.0 * k
                for f in range(fields):
                    c = s[i + 1, f, at : at + BLK, :]
                    new = (
                        k_c * c
                        + k_e * s[i + 1, f, at + 1 : at + 1 + BLK, :]
                        + k_w * s[i + 1, f, at - 1 : at - 1 + BLK, :]
                        + k_n * s[i + 2, f, at : at + BLK, :]
                        + k_s * s[i, f, at : at + BLK, :]
                        + vertical(c)
                    )
                    if keep is not None:
                        keep[i + 1, f, at : at + BLK, :] = new
                    cols[slot, i * halves + h, :, f * levels : (f + 1) * levels] = new.astype(BF16)

    def dispatch(slot, blocks, sent, got, send_sem, recv_sem):
        got[slot, 0] = blocks[slot, pick[slot, 0]]
        for k in range(1, n_lon):
            sent[slot, k] = blocks[slot, pick[slot, k]]
            remote(
                sent.at[slot, k], got.at[slot, k], send_sem.at[slot],
                recv_sem.at[slot, k // chunk], to(k),
            ).start()

    loads[0].wait()
    send_state(0, s0)
    loads[2].wait()
    dispatch(1, rst, send_r, recv_r, rs_sem, rr_sem)
    loads[1].wait()
    take_state(0, s0)
    advance(s0, 0, s1)
    send_state(1, s1)
    dispatch(0, rst, send_r, recv_r, rs_sem, rr_sem)
    take_state(1, s1)
    advance(s1, 1, None)
    dispatch(1, cols, send_c, recv_c, cs_sem, cr_sem)
    dispatch(0, cols, send_c, recv_c, cs_sem, cr_sem)
    for load in loads[3:]:
        load.wait()

    span = chunk * BLK
    h1, h2, ch, cin = w1.shape[1], w2.shape[1], w3.shape[1], w1.shape[0]

    def tiles(n):
        return [slice(a, min(a + TILE, n)) for a in range(0, n, TILE)]

    def nn(a, b):
        return lax.dot_general(a, b, (((1,), (0,)), ((), ())), preferred_element_type=F32)

    def nt(a, b):
        return lax.dot_general(a, b, (((1,), (1,)), ((), ())), preferred_element_type=F32)

    def activate(z):
        sig = 0.5 * jnp.tanh(0.5 * z) + 0.5
        act = z * sig
        return act.astype(BF16), sig + act * (1.0 - sig)

    def wait_chunk(got, sem, slot, g):
        for first in (True, False):
            @pl.when((g == 0) if first else (g > 0))
            def _():
                part = got.at[slot, pl.ds(1, chunk - 1)] if first else got.at[slot, pl.ds(g * chunk, chunk)]
                pltpu.make_async_copy(part, part, sem.at[slot, g]).wait()

    @pl.loop(0, 2 * chunks)
    def _(t):
        slot = 1 - t // chunks
        g = lax.rem(t, chunks)
        base = g * chunk
        wait_chunk(recv_r, rr_sem, slot, g)
        wait_chunk(recv_c, cr_sem, slot, g)
        for n in tiles(h1):
            x = recv_c[slot, pl.ds(base, chunk)].reshape(span, cin)
            a1[:, n], g1[:, n] = activate(nn(x, w1[:, n]))
        for n in tiles(h2):
            a2[:, n], g2[:, n] = activate(nn(a1[...], w2[:, n]))
        for n in tiles(ch):
            y = recv_r[slot, pl.ds(base, chunk), :, n].reshape(span, n.stop - n.start).astype(F32)
            mis[:, n] = (cw[:, n] * (nn(a2[...], w3[:, n]) - y)).astype(BF16)
        for n in tiles(h2):
            gg2[:, n] = (nt(mis[...], w3[n, :]) * g2[:, n]).astype(BF16)
        for n in tiles(h1):
            gg1[:, n] = (nt(gg2[...], w2[n, :]) * g1[:, n]).astype(BF16)
        for n in tiles(cin):
            rep_s[slot, pl.ds(base, chunk), :, n] = (
                nt(gg1[...], w1[n, :]).astype(BF16).reshape(chunk, BLK, n.stop - n.start)
            )
        for tt in range(2 * chunks):
            @pl.when(t == tt)
            def _():
                home, replies = 1 - tt // chunks, rep_r[1 - tt // chunks]
                for k in range(tt % chunks * chunk, (tt % chunks + 1) * chunk):
                    if k == 0:
                        replies[0] = rep_s[home, 0]
                    else:
                        remote(
                            rep_s.at[home, k], replies.at[k], ps_sem.at[home],
                            pr_sem.at[home], back(k),
                        ).start()


    def wait_replies(slot):
        part = rep_r[slot].at[pl.ds(1, n_lon - 1)]
        pltpu.make_async_copy(part, part, pr_sem.at[slot]).wait()

    def unpack(slot):
        @pl.loop(0, rows)
        def _(i):
            for h in range(halves):
                k = slotk[slot, i * halves + h]
                for f in range(fields):
                    frc[i, f, h * BLK : (h + 1) * BLK, :] = rep_r[slot][
                        k, :, f * levels : (f + 1) * levels
                    ].astype(F32)

    def flux_rows(phase, s, i):
        for h in range(halves):
            part = slice(h * BLK, (h + 1) * BLK)
            k = kap[i, part, :]
            v = ADVECT * s[i + 1, 1, PAD + h * BLK : PAD + (h + 1) * BLK, :]
            k_n, k_s = k - v, k + v
            for f in range(fields):
                g = frc[i, f, part, :]
                north[phase - 2, i + 1, f, part, :] = g * k_n
                south[phase - 2, i, f, part, :] = g * k_s

    def adjoint_rows(phase):
        n, s = north.at[phase - 2], south.at[phase - 2]
        return (n.at[rows], n.at[0], s.at[0], s.at[rows])

    def send_adjoint(phase, s):
        flux_rows(phase, s, 0)
        flux_rows(phase, s, rows - 1)
        send_rows(phase, *adjoint_rows(phase))

        @pl.loop(0, rows)
        def _(i):
            for side, j in ((0, width - 1), (1, 0)):
                k = kap[i, j : j + 1, :]
                u = ADVECT * s[i + 1, 0, PAD + j : PAD + j + 1, :]
                coef = k - u if side == 0 else k + u
                for f in range(fields):
                    edge_s[phase, side, i, f : f + 1, :] = coef * frc[i, f, j : j + 1, :]

        send_edges(phase)

        @pl.loop(1, rows - 1)
        def _(i):
            flux_rows(phase, s, i)

    def local_adjoint(s):
        for f in range(fields):
            flux[0, f, 0:PAD, :] = jnp.zeros((PAD, levels), F32)
            flux[1, f, PAD + width :, :] = jnp.zeros((PAD, levels), F32)

        @pl.loop(0, rows)
        def _(i):
            for h in range(halves):
                at = PAD + h * BLK
                k = kap[i, h * BLK : (h + 1) * BLK, :]
                u = ADVECT * s[i + 1, 0, at : at + BLK, :]
                k_e, k_w = k - u, k + u
                for f in range(fields):
                    g = frc[i, f, h * BLK : (h + 1) * BLK, :]
                    flux[0, f, at : at + BLK, :] = k_e * g
                    flux[1, f, at : at + BLK, :] = k_w * g
            for h in range(halves):
                part = slice(h * BLK, (h + 1) * BLK)
                at = PAD + h * BLK
                k_c = (1.0 - 2.0 * VERTICAL) - 4.0 * kap[i, part, :]
                zonal = jnp.zeros((BLK, levels), F32)
                merid = jnp.zeros((BLK, levels), F32)
                for f in reversed(range(fields)):
                    g = frc[i, f, part, :]
                    zonal += g * (s[i + 1, f, at + 1 : at + 1 + BLK, :] - s[i + 1, f, at - 1 : at - 1 + BLK, :])
                    merid += g * (s[i + 2, f, at : at + BLK, :] - s[i, f, at : at + BLK, :])
                    own = (
                        k_c * g + vertical(g)
                        + flux[0, f, at - 1 : at - 1 + BLK, :] + flux[1, f, at + 1 : at + 1 + BLK, :]
                    )
                    acc[i, f, part, :] = own
                acc[i, 0, part, :] -= ADVECT * zonal
                acc[i, 1, part, :] -= ADVECT * merid

    def finish_adjoint(phase, done):
        wait_halo(phase, *adjoint_rows(phase))

        @pl.when(lat == 0)
        def _():
            north[phase - 2, 0] = jnp.zeros((fields, width, levels), F32)

        @pl.when(lat == n_lat - 1)
        def _():
            south[phase - 2, rows] = jnp.zeros((fields, width, levels), F32)

        @pl.loop(0, rows)
        def _(i):
            for f in range(fields):
                acc[i, f, 0:1, :] += edge_r[phase, 0, i, f : f + 1, :]
                acc[i, f, width - 1 : width, :] += edge_r[phase, 1, i, f : f + 1, :]
            for h in range(halves):
                part = slice(h * BLK, (h + 1) * BLK)
                for f in range(fields):
                    total = acc[i, f, part, :] + north[phase - 2, i, f, part, :] + south[phase - 2, i + 1, f, part, :]
                    done(i, h, f, part, total)

    def to_costate(i, h, f, part, total):
        forced = rep_0[slotk[0, i * halves + h], :, f * levels : (f + 1) * levels]
        frc[i, f, part, :] = forced.astype(F32) + total

    def to_gradient(i, h, f, part, total):
        own = s0[i + 1, f, PAD + part.start : PAD + part.stop, :]
        acc[i, f, part, :] = (own - bgv[i, f, part, :]) + total
        if h == halves - 1 and f == fields - 1:
            pltpu.make_async_copy(acc.at[i], out.at[i], out_sem).start()

    wait_replies(1)
    unpack(1)
    send_adjoint(2, s1)
    local_adjoint(s1)
    wait_replies(0)
    finish_adjoint(2, to_costate)
    send_adjoint(3, s0)
    local_adjoint(s0)
    finish_adjoint(3, to_gradient)

    for slot in (0, 1):
        for buffer, sem in ((send_r, rs_sem), (send_c, cs_sem), (rep_s, ps_sem)):
            part = buffer.at[slot, pl.ds(1, n_lon - 1)]
            pltpu.make_async_copy(part, part, sem.at[slot]).wait()
    pltpu.make_async_copy(acc, out, out_sem).wait()


def shards(state, background, diffusivity, radiances, owners, first, second, third, weight):
    n_lon, n_lat = lax.axis_size("lon"), lax.axis_size("lat")
    rows, width, fields, levels = state.shape
    blocks = owners.shape[2]
    channels = radiances.shape[3]
    cin, h1, h2 = first.shape[1], first.shape[2], second.shape[2]
    nz, ny = torus(n_lon)
    order = offset_order(n_lon)
    chunk = min(CHUNK, n_lon // 4)
    span = chunk * BLK

    lon = lax.axis_index("lon")
    peers = jnp.stack(
        [
            lax.rem(lon // (2 * ny) + a, nz) * (2 * ny) + lax.rem(lax.rem(lon // 2, ny) + b, ny) * 2 + lax.rem(lon + c, 2)
            for a, b, c in order
        ]
    )
    owner = owners[:, 0, :]
    match = owner[:, None, :] == peers[None, :, None]
    pick = jnp.sum(jnp.where(match, jnp.arange(blocks, dtype=jnp.int32)[None, None, :], 0), axis=2)
    slotk = jnp.sum(jnp.where(match, jnp.arange(n_lon, dtype=jnp.int32)[None, :, None], 0), axis=1)

    smem = pl.BlockSpec(memory_space=pltpu.SMEM)
    hbm = pl.BlockSpec(memory_space=pl.ANY)
    dma = pltpu.SemaphoreType.DMA
    body = functools.partial(kernel, n_lon, n_lat)
    slots = 2
    field = (rows, fields, width, levels)
    result = pl.pallas_call(
        body,
        out_shape=jax.ShapeDtypeStruct(field, F32),
        in_specs=[smem, smem] + [hbm] * 8,
        out_specs=hbm,
        scratch_shapes=[
            pltpu.VMEM((rows + 2, fields, width + 2 * PAD, levels), F32),
            pltpu.VMEM((rows + 2, fields, width + 2 * PAD, levels), F32),
            pltpu.VMEM((rows, width, levels), F32),
            pltpu.VMEM((slots, blocks, BLK, channels), BF16),
            pltpu.VMEM((slots, blocks, BLK, cin), BF16),
            pltpu.VMEM((slots, n_lon, BLK, channels), BF16),
            pltpu.VMEM((slots, n_lon, BLK, cin), BF16),
            pltpu.VMEM((slots, n_lon, BLK, channels), BF16),
            pltpu.VMEM((slots, n_lon, BLK, cin), BF16),
            pltpu.VMEM((slots, n_lon, BLK, cin), BF16),
            pltpu.VMEM((n_lon, BLK, cin), BF16),
            pltpu.VMEM((n_lon, BLK, cin), BF16),
            pltpu.VMEM((cin, h1), BF16),
            pltpu.VMEM((h1, h2), BF16),
            pltpu.VMEM((h2, channels), BF16),
            pltpu.VMEM((1, channels), F32),
            pltpu.VMEM(field, F32),
            pltpu.VMEM(field, F32),
            pltpu.VMEM(field, F32),
            pltpu.VMEM((2, rows + 1, fields, width, levels), F32),
            pltpu.VMEM((2, rows + 1, fields, width, levels), F32),
            pltpu.VMEM((2, fields, width + 2 * PAD, levels), F32),
            pltpu.VMEM((4, 2, rows, 8, levels), F32),
            pltpu.VMEM((4, 2, rows, 8, levels), F32),
            pltpu.VMEM((span, h1), BF16),
            pltpu.VMEM((span, h1), F32),
            pltpu.VMEM((span, h2), BF16),
            pltpu.VMEM((span, h2), F32),
            pltpu.VMEM((span, channels), BF16),
            pltpu.VMEM((span, h2), BF16),
            pltpu.VMEM((span, h1), BF16),
            dma((8,)),
            dma,
            dma((slots,)),
            dma((slots, n_lon // chunk)),
            dma((slots,)),
            dma((slots, n_lon // chunk)),
            dma((slots,)),
            dma((slots,)),
            dma((4, 2)),
            dma((4, 2)),
            dma((4, 2)),
            dma((4, 2)),
        ],
        compiler_params=pltpu.CompilerParams(
            collective_id=0, has_side_effects=True, vmem_limit_bytes=56 * 2**20
        ),
        name="gradient",
    )(
        pick,
        slotk,
        state.transpose(0, 2, 1, 3),
        background.transpose(0, 2, 1, 3),
        diffusivity,
        radiances.reshape(slots, blocks, BLK, channels),
        first[0],
        second[0],
        third[0],
        weight,
    )
    return result.transpose(0, 2, 1, 3)


def solution(mesh):
    placed = (
        P("lat", "lon", None, None),
        P("lat", "lon", None, None),
        P("lat", "lon", None),
        P(None, "lat", "lon", None),
        P(None, "lat", "lon"),
        P("lon", None, None),
        P("lon", None, None),
        P("lon", None, None),
        P("lon", None),
    )
    return jax.shard_map(
        shards, mesh=mesh, in_specs=placed, out_specs=P("lat", "lon", None, None), check_vma=False
    )
```

```python
import functools

import jax
import jax.numpy as jnp
from jax import lax
from jax.experimental import pallas as pl
from jax.experimental.pallas import tpu as pltpu
from jax.sharding import PartitionSpec as P

MESH = pl.DeviceIdType.MESH
F32 = jnp.float32
BF16 = jnp.bfloat16
ADVECT = 0.125
VERTICAL = 0.1
BLK = 32
CHUNK = 8
TILE = 256
PAD = 8


def torus(n_lon):
    chips = n_lon // 2
    ny = 1
    while ny * ny < chips:
        ny *= 2
    return chips // ny, ny


def offset_order(n_lon):
    nz, ny = torus(n_lon)

    def hops(d):
        return min(d[0], nz - d[0]) + min(d[1], ny - d[1])

    chips = []
    for d in sorted(((a, b) for a in range(nz) for b in range(ny) if a or b), key=lambda d: (hops(d), d)):
        opposite = ((nz - d[0]) % nz, (ny - d[1]) % ny)
        for e in (d, opposite):
            if e not in chips:
                chips.append(e)
    return [(0, 0, 0), (0, 0, 1)] + [(a, b, c) for c in (0, 1) for a, b in chips]


def kernel(
    n_lon, n_lat, own_h,
    st, bg, kd, rad, w1h, w2h, w3h, cwh,
    acc,
    s0, s1, kap, rst, cols, send_r, send_c, recv_r, recv_c, rep_s, rep_0, rep_1,
    w1, w2, w3, cw, bgv, frc_a, frc_b, rim_s, rim_r, flux, edge_s, edge_r, own, pick, slotk, place,
    a1, g1, a2, g2, mis, gg2, gg1,
    load_sem, cs_sem, cr_sem, rs_sem, rr_sem, ps_sem, pr_sem,
    ns_s, ns_r, ew_s, ew_r,
):
    rows, fields, width, levels = st.shape
    halves = width // BLK
    nz, ny = torus(n_lon)
    order = offset_order(n_lon)
    chunk = min(CHUNK, n_lon // 4)
    chunks = n_lon // chunk
    lon = lax.axis_index("lon")
    lat = lax.axis_index("lat")
    core = lax.rem(lon, 2)
    yy = lax.rem(lon // 2, ny)
    zz = lon // (2 * ny)
    z_at = [lax.rem(zz + d, nz) * (2 * ny) for d in range(nz)]
    y_at = [lax.rem(yy + d, ny) * 2 for d in range(ny)]
    c_at = [core, 1 - core]

    rep_r = (rep_0, rep_1)

    def to(k):
        a, b, c = order[k]
        return (z_at[a] + y_at[b] + c_at[c], lat)

    def back(k):
        a, b, c = order[k]
        return (z_at[(nz - a) % nz] + y_at[(ny - b) % ny] + c_at[c], lat)

    up = (lon, lax.rem(lat + 1, n_lat))
    down = (lon, lax.rem(lat + n_lat - 1, n_lat))
    east = (lax.rem(lon + 1, n_lon), lat)
    west = (lax.rem(lon + n_lon - 1, n_lon), lat)
    inner = pl.ds(PAD, width)

    loads = [
        (st, s0.at[pl.ds(1, rows), :, inner, :]), (rad.at[1], rst.at[1]), (kd, kap.at[pl.ds(1, rows)]),
        (rad.at[0], rst.at[0]), (own_h, own), (w1h, w1), (w2h, w2), (w3h, w3), (cwh, cw), (bg, bgv),
    ]
    loads = [pltpu.make_async_copy(src, dst, load_sem.at[i]) for i, (src, dst) in enumerate(loads)]
    for load in loads[:5]:
        load.start()

    barrier = pltpu.get_barrier_semaphore()
    for k in range(1, n_lon):
        pl.semaphore_signal(barrier, inc=1, device_id=to(k), device_id_type=MESH)
    for there in (up, down):
        pl.semaphore_signal(barrier, inc=1, device_id=there, device_id_type=MESH)
    for load in loads[5:]:
        load.start()

    for k, (a, b, c) in enumerate(order):
        place[(a * ny + b) * 2 + c] = k

    def find_blocks(slot):
        found = []
        for b in range(own.shape[2]):
            owner = own[slot, 0, b]
            a = lax.rem(owner // (2 * ny) - zz + nz, nz)
            d = lax.rem(lax.rem(owner // 2, ny) - yy + ny, ny)
            c = lax.rem(lax.rem(owner, 2) + core, 2)
            found.append(place[(a * ny + d) * 2 + c])
            slotk[slot, b] = found[-1]

        @pl.loop(0, n_lon)
        def _(k):
            block = jnp.int32(0)
            for b, at in enumerate(found):
                block = jnp.where(at == k, b, block)
            pick[slot, k] = block

    def remote(src, dst, send_sem, recv_sem, there):
        return pltpu.make_async_remote_copy(
            src_ref=src, dst_ref=dst, send_sem=send_sem, recv_sem=recv_sem,
            device_id=there, device_id_type=MESH,
        )

    def send_rows(phase, row_up, to_up, row_down, to_down):
        remote(row_up, to_up, ns_s.at[phase, 0], ns_r.at[phase, 0], up).start()
        remote(row_down, to_down, ns_s.at[phase, 1], ns_r.at[phase, 1], down).start()

    def send_edges(phase):
        for side, there in ((0, east), (1, west)):
            remote(
                edge_s.at[phase, side], edge_r.at[phase, side],
                ew_s.at[phase, side], ew_r.at[phase, side], there,
            ).start()

    def wait_rows(phase, row_up, to_up, row_down, to_down):
        remote(row_up, to_up, ns_s.at[phase, 0], ns_r.at[phase, 0], up).wait()
        remote(row_down, to_down, ns_s.at[phase, 1], ns_r.at[phase, 1], down).wait()

    def wait_edges(phase):
        for side, there in ((0, east), (1, west)):
            remote(
                edge_s.at[phase, side], edge_r.at[phase, side],
                ew_s.at[phase, side], ew_r.at[phase, side], there,
            ).wait()

    def state_rows(s):
        return (
            s.at[rows, :, inner, :], s.at[0, :, inner, :],
            s.at[1, :, inner, :], s.at[rows + 1, :, inner, :],
        )

    def pack_state(phase, s):
        @pl.loop(0, rows)
        def _(i):
            for f in range(fields):
                edge_s[phase, 0, i, f : f + 1, :] = s[i + 1, f, PAD + width - 1 : PAD + width, :]
                edge_s[phase, 1, i, f : f + 1, :] = s[i + 1, f, PAD : PAD + 1, :]

    def send_state(phase, s):
        send_rows(phase, *state_rows(s))
        send_edges(phase)

    def take_state(phase, s):
        wait_rows(phase, *state_rows(s))
        wait_edges(phase)

        @pl.loop(0, rows)
        def _(i):
            for f in range(fields):
                s[i + 1, f, PAD - 1 : PAD, :] = edge_r[phase, 0, i, f : f + 1, :]
                s[i + 1, f, PAD + width : PAD + width + 1, :] = edge_r[phase, 1, i, f : f + 1, :]

        @pl.when(lat == 0)
        def _():
            s[0, :, PAD : PAD + width, :] = jnp.zeros((fields, width, levels), F32)

        @pl.when(lat == n_lat - 1)
        def _():
            s[rows + 1, :, PAD : PAD + width, :] = jnp.zeros((fields, width, levels), F32)

    level = lax.broadcasted_iota(jnp.int32, (BLK, levels), 1)
    from_below = jnp.where(level == 0, 0.0, VERTICAL).astype(F32)
    from_above = jnp.where(level == levels - 1, 0.0, VERTICAL).astype(F32)

    def vertical(v):
        return from_below * pltpu.roll(v, 1, 1) + from_above * pltpu.roll(v, levels - 1, 1)

    def advance(s, slot, keep):
        @pl.loop(0, rows)
        def _(i):
            for h in range(halves):
                at = PAD + h * BLK
                k = kap[i + 1, h * BLK : (h + 1) * BLK, :]
                u = ADVECT * s[i + 1, 0, at : at + BLK, :]
                v = ADVECT * s[i + 1, 1, at : at + BLK, :]
                k_e, k_w, k_n, k_s = k - u, k + u, k - v, k + v
                k_c = (1.0 - 2.0 * VERTICAL) - 4.0 * k
                for f in range(fields):
                    c = s[i + 1, f, at : at + BLK, :]
                    new = (
                        k_c * c
                        + k_e * s[i + 1, f, at + 1 : at + 1 + BLK, :]
                        + k_w * s[i + 1, f, at - 1 : at - 1 + BLK, :]
                        + k_n * s[i + 2, f, at : at + BLK, :]
                        + k_s * s[i, f, at : at + BLK, :]
                        + vertical(c)
                    )
                    if keep is not None:
                        keep[i + 1, f, at : at + BLK, :] = new
                    cols[slot, i * halves + h, :, f * levels : (f + 1) * levels] = new.astype(BF16)

    def pack(slot, blocks, sent, got):
        got[slot, 0] = blocks[slot, pick[slot, 0]]
        for k in range(1, n_lon):
            sent[slot, k] = blocks[slot, pick[slot, k]]

    def dispatch(slot, sent, got, send_sem, recv_sem):
        for k in range(1, n_lon):
            remote(
                sent.at[slot, k], got.at[slot, k], send_sem.at[slot],
                recv_sem.at[slot, k // chunk], to(k),
            ).start()

    def send_columns(slot):
        recv_c[slot, 0] = cols[slot, pick[slot, 0]]
        for k in range(1, n_lon):
            send_c[slot, k] = cols[slot, pick[slot, k]]
            remote(
                send_c.at[slot, k], recv_c.at[slot, k], cs_sem.at[slot],
                cr_sem.at[slot, k // chunk], to(k),
            ).start()

    loads[4].wait()
    find_blocks(1)
    loads[0].wait()
    pack_state(0, s0)
    loads[1].wait()
    loads[3].wait()
    pack(1, rst, send_r, recv_r)
    pl.semaphore_wait(barrier, n_lon + 1)
    send_state(0, s0)
    dispatch(1, send_r, recv_r, rs_sem, rr_sem)
    find_blocks(0)
    pack(0, rst, send_r, recv_r)
    dispatch(0, send_r, recv_r, rs_sem, rr_sem)
    loads[2].wait()
    take_state(0, s0)
    advance(s0, 0, s1)
    pack_state(1, s1)
    send_state(1, s1)
    take_state(1, s1)
    advance(s1, 1, None)
    send_columns(1)
    send_columns(0)
    for load in loads[5:]:
        load.wait()

    @pl.loop(0, rows)
    def _(i):
        for f in range(fields):
            bgv[i, f] = s0[i + 1, f, PAD : PAD + width, :] - bgv[i, f]

    for i in (0, rows + 1):
        kap[i] = jnp.zeros((width, levels), F32)
        frc_a[i] = jnp.zeros((fields, width, levels), F32)
        frc_b[i] = jnp.zeros((fields, width, levels), F32)

    span = chunk * BLK
    h1, h2, ch, cin = w1.shape[1], w2.shape[1], w3.shape[1], w1.shape[0]

    def tiles(n):
        return [slice(a, min(a + TILE, n)) for a in range(0, n, TILE)]

    def nn(a, b):
        return lax.dot_general(a, b, (((1,), (0,)), ((), ())), preferred_element_type=F32)

    def nt(a, b):
        return lax.dot_general(a, b, (((1,), (1,)), ((), ())), preferred_element_type=F32)

    def activate(z):
        sig = 0.5 * jnp.tanh(0.5 * z) + 0.5
        act = z * sig
        return act.astype(BF16), sig + act * (1.0 - sig)

    def wait_chunk(got, sem, slot, g):
        for first in (True, False):
            @pl.when((g == 0) if first else (g > 0))
            def _():
                part = got.at[slot, pl.ds(1, chunk - 1)] if first else got.at[slot, pl.ds(g * chunk, chunk)]
                pltpu.make_async_copy(part, part, sem.at[slot, g]).wait()

    @pl.loop(0, 2 * chunks)
    def _(t):
        slot = 1 - t // chunks
        g = lax.rem(t, chunks)
        base = g * chunk
        wait_chunk(recv_r, rr_sem, slot, g)
        wait_chunk(recv_c, cr_sem, slot, g)
        for n in tiles(h1):
            x = recv_c[slot, pl.ds(base, chunk)].reshape(span, cin)
            a1[:, n], g1[:, n] = activate(nn(x, w1[:, n]))
        for n in tiles(h2):
            a2[:, n], g2[:, n] = activate(nn(a1[...], w2[:, n]))
        for n in tiles(ch):
            y = recv_r[slot, pl.ds(base, chunk), :, n].reshape(span, n.stop - n.start).astype(F32)
            mis[:, n] = (cw[:, n] * (nn(a2[...], w3[:, n]) - y)).astype(BF16)
        for n in tiles(h2):
            gg2[:, n] = (nt(mis[...], w3[n, :]) * g2[:, n]).astype(BF16)
        for n in tiles(h1):
            gg1[:, n] = (nt(gg2[...], w2[n, :]) * g1[:, n]).astype(BF16)
        for n in tiles(cin):
            rep_s[slot, pl.ds(base, chunk), :, n] = (
                nt(gg1[...], w1[n, :]).astype(BF16).reshape(chunk, BLK, n.stop - n.start)
            )
        for tt in range(2 * chunks):
            @pl.when(t == tt)
            def _():
                home, replies = 1 - tt // chunks, rep_r[1 - tt // chunks]
                for k in range(tt % chunks * chunk, (tt % chunks + 1) * chunk):
                    if k == 0:
                        replies[0] = rep_s[home, 0]
                    else:
                        remote(
                            rep_s.at[home, k], replies.at[k], ps_sem.at[home],
                            pr_sem.at[home], back(k),
                        ).start()


    def wait_replies(slot):
        part = rep_r[slot].at[pl.ds(1, n_lon - 1)]
        pltpu.make_async_copy(part, part, pr_sem.at[slot]).wait()

    def forced(slot, i, h, f):
        return rep_r[slot][slotk[slot, i * halves + h], :, f * levels : (f + 1) * levels].astype(F32)

    def rims(phase):
        out_rim, in_rim = rim_s.at[phase - 2], rim_r.at[phase - 2]
        return (out_rim.at[0], in_rim.at[0], out_rim.at[1], in_rim.at[1])

    def send_rims(phase, s, g):
        for side, i, sign in ((0, rows, -1.0), (1, 1, 1.0)):
            for h in range(halves):
                part = slice(h * BLK, (h + 1) * BLK)
                coef = kap[i, part, :] + (sign * ADVECT) * s[i, 1, PAD + h * BLK : PAD + (h + 1) * BLK, :]
                for f in range(fields):
                    rim_s[phase - 2, side, f, part, :] = (coef * g[i, f, part, :]).astype(BF16)
        send_rows(phase, *rims(phase))

    def send_sides(phase, s, g):
        @pl.loop(0, rows)
        def _(i):
            for side, j, sign in ((0, width - 1, -1.0), (1, 0, 1.0)):
                coef = kap[i + 1, j : j + 1, :] + (sign * ADVECT) * s[i + 1, 0, PAD + j : PAD + j + 1, :]
                for f in range(fields):
                    edge_s[phase, side, i, f : f + 1, :] = coef * g[i + 1, f, j : j + 1, :]

        send_edges(phase)

    for f in range(fields):
        flux[0, f, 0:PAD, :] = jnp.zeros((PAD, levels), F32)
        flux[1, f, PAD + width :, :] = jnp.zeros((PAD, levels), F32)

    def transpose_tile(s, g, into, shift, extra):
        @pl.loop(0, rows)
        def _(i):
            for h in range(halves):
                at = PAD + h * BLK
                k = kap[i + 1, h * BLK : (h + 1) * BLK, :]
                u = ADVECT * s[i + 1, 0, at : at + BLK, :]
                k_e, k_w = k - u, k + u
                for f in range(fields):
                    own_g = g[i + 1, f, h * BLK : (h + 1) * BLK, :]
                    flux[0, f, at : at + BLK, :] = k_e * own_g
                    flux[1, f, at : at + BLK, :] = k_w * own_g
            for h in range(halves):
                part = slice(h * BLK, (h + 1) * BLK)
                at = PAD + h * BLK
                k_c = (1.0 - 2.0 * VERTICAL) - 4.0 * kap[i + 1, part, :]
                k_n = kap[i, part, :] - ADVECT * s[i, 1, at : at + BLK, :]
                k_s = kap[i + 2, part, :] + ADVECT * s[i + 2, 1, at : at + BLK, :]
                zonal = jnp.zeros((BLK, levels), F32)
                merid = jnp.zeros((BLK, levels), F32)
                for f in reversed(range(fields)):
                    own_g = g[i + 1, f, part, :]
                    zonal += own_g * (
                        s[i + 1, f, at + 1 : at + 1 + BLK, :] - s[i + 1, f, at - 1 : at - 1 + BLK, :]
                    )
                    merid += own_g * (s[i + 2, f, at : at + BLK, :] - s[i, f, at : at + BLK, :])
                    total = (
                        k_c * own_g + vertical(own_g)
                        + k_n * g[i, f, part, :] + k_s * g[i + 2, f, part, :]
                        + flux[0, f, at - 1 : at - 1 + BLK, :] + flux[1, f, at + 1 : at + 1 + BLK, :]
                    )
                    if extra is not None:
                        total += extra[i, f, part, :]
                    if f == 0:
                        total -= ADVECT * zonal
                    into[i + shift, f, part, :] = total
                into[i + shift, 1, part, :] -= ADVECT * merid

    def add_sides(phase, into, shift):
        wait_edges(phase)

        @pl.loop(0, rows)
        def _(i):
            for f in range(fields):
                into[i + shift, f, 0:1, :] += edge_r[phase, 0, i, f : f + 1, :]
                into[i + shift, f, width - 1 : width, :] += edge_r[phase, 1, i, f : f + 1, :]

    def add_rims(phase, into, shift):
        wait_rows(phase, *rims(phase))
        for side, i, there in ((0, 0, lat > 0), (1, rows - 1, lat < n_lat - 1)):
            @pl.when(there)
            def _():
                for f in range(fields):
                    into[i + shift, f] += rim_r[phase - 2, side, f].astype(F32)

    def add_forced(i):
        for h in range(halves):
            for f in range(fields):
                frc_b[i + 1, f, h * BLK : (h + 1) * BLK, :] += forced(0, i, h, f)

    wait_replies(1)

    @pl.loop(0, rows)
    def _(i):
        for h in range(halves):
            for f in range(fields):
                frc_a[i + 1, f, h * BLK : (h + 1) * BLK, :] = forced(1, i, h, f)

    send_rims(2, s1, frc_a)
    send_sides(2, s1, frc_a)
    transpose_tile(s1, frc_a, frc_b, 1, None)
    add_sides(2, frc_b, 1)
    add_rims(2, frc_b, 1)

    wait_replies(0)
    add_forced(0)
    add_forced(rows - 1)
    send_rims(3, s0, frc_b)
    pl.loop(1, rows - 1)(add_forced)
    send_sides(3, s0, frc_b)
    transpose_tile(s0, frc_b, acc, 0, bgv)
    add_sides(3, acc, 0)
    add_rims(3, acc, 0)

    for slot in (0, 1):
        for buffer, sem in ((send_r, rs_sem), (send_c, cs_sem), (rep_s, ps_sem)):
            part = buffer.at[slot, pl.ds(1, n_lon - 1)]
            pltpu.make_async_copy(part, part, sem.at[slot]).wait()


def shards(state, background, diffusivity, radiances, owners, first, second, third, weight):
    n_lon, n_lat = lax.axis_size("lon"), lax.axis_size("lat")
    rows, width, fields, levels = state.shape
    blocks = owners.shape[2]
    channels = radiances.shape[3]
    cin, h1, h2 = first.shape[1], first.shape[2], second.shape[2]
    chunk = min(CHUNK, n_lon // 4)
    span = chunk * BLK

    hbm = pl.BlockSpec(memory_space=pltpu.HBM)
    dma = pltpu.SemaphoreType.DMA
    body = functools.partial(kernel, n_lon, n_lat)
    slots = 2
    field = (rows, fields, width, levels)
    result = pl.pallas_call(
        body,
        out_shape=pltpu.VMEM(field, F32),
        in_specs=[hbm] * 9,
        out_specs=pl.BlockSpec(memory_space=pltpu.VMEM),
        scratch_shapes=[
            pltpu.VMEM((rows + 2, fields, width + 2 * PAD, levels), F32),
            pltpu.VMEM((rows + 2, fields, width + 2 * PAD, levels), F32),
            pltpu.VMEM((rows + 2, width, levels), F32),
            pltpu.VMEM((slots, blocks, BLK, channels), BF16),
            pltpu.VMEM((slots, blocks, BLK, cin), BF16),
            pltpu.VMEM((slots, n_lon, BLK, channels), BF16),
            pltpu.VMEM((slots, n_lon, BLK, cin), BF16),
            pltpu.VMEM((slots, n_lon, BLK, channels), BF16),
            pltpu.VMEM((slots, n_lon, BLK, cin), BF16),
            pltpu.VMEM((slots, n_lon, BLK, cin), BF16),
            pltpu.VMEM((n_lon, BLK, cin), BF16),
            pltpu.VMEM((n_lon, BLK, cin), BF16),
            pltpu.VMEM((cin, h1), BF16),
            pltpu.VMEM((h1, h2), BF16),
            pltpu.VMEM((h2, channels), BF16),
            pltpu.VMEM((1, channels), F32),
            pltpu.VMEM(field, F32),
            pltpu.VMEM((rows + 2, fields, width, levels), F32),
            pltpu.VMEM((rows + 2, fields, width, levels), F32),
            pltpu.VMEM((2, 2, fields, width, levels), BF16),
            pltpu.VMEM((2, 2, fields, width, levels), BF16),
            pltpu.VMEM((2, fields, width + 2 * PAD, levels), F32),
            pltpu.VMEM((4, 2, rows, 8, levels), F32),
            pltpu.VMEM((4, 2, rows, 8, levels), F32),
            pltpu.SMEM((slots, 1, blocks), jnp.int32),
            pltpu.SMEM((slots, n_lon), jnp.int32),
            pltpu.SMEM((slots, blocks), jnp.int32),
            pltpu.SMEM((n_lon,), jnp.int32),
            pltpu.VMEM((span, h1), BF16),
            pltpu.VMEM((span, h1), F32),
            pltpu.VMEM((span, h2), BF16),
            pltpu.VMEM((span, h2), F32),
            pltpu.VMEM((span, channels), BF16),
            pltpu.VMEM((span, h2), BF16),
            pltpu.VMEM((span, h1), BF16),
            dma((10,)),
            dma((slots,)),
            dma((slots, n_lon // chunk)),
            dma((slots,)),
            dma((slots, n_lon // chunk)),
            dma((slots,)),
            dma((slots,)),
            dma((4, 2)),
            dma((4, 2)),
            dma((4, 2)),
            dma((4, 2)),
        ],
        compiler_params=pltpu.CompilerParams(
            collective_id=0, has_side_effects=True, vmem_limit_bytes=60 * 2**20
        ),
        name="gradient",
    )(
        owners,
        state.transpose(0, 2, 1, 3),
        background.transpose(0, 2, 1, 3),
        diffusivity,
        radiances.reshape(slots, blocks, BLK, channels),
        first[0],
        second[0],
        third[0],
        weight,
    )
    return result.transpose(0, 2, 1, 3)


def solution(mesh):
    placed = (
        P("lat", "lon", None, None),
        P("lat", "lon", None, None),
        P("lat", "lon", None),
        P(None, "lat", "lon", None),
        P(None, "lat", "lon"),
        P("lon", None, None),
        P("lon", None, None),
        P("lon", None, None),
        P("lon", None),
    )
    return jax.shard_map(
        shards, mesh=mesh, in_specs=placed, out_specs=P("lat", "lon", None, None), check_vma=False
    )
```

```python
import functools

import jax
import jax.numpy as jnp
from jax import lax
from jax.experimental import pallas as pl
from jax.experimental.pallas import tpu as pltpu
from jax.sharding import PartitionSpec as P

MESH = pl.DeviceIdType.MESH
F32 = jnp.float32
BF16 = jnp.bfloat16
ADVECT = 0.125
VERTICAL = 0.1
BLK = 32
CHUNK = 8
TILE = 256
PAD = 8


def torus(n_lon):
    chips = n_lon // 2
    ny = 1
    while ny * ny < chips:
        ny *= 2
    return chips // ny, ny


def offset_order(n_lon):
    nz, ny = torus(n_lon)

    def hops(d):
        return min(d[0], nz - d[0]) + min(d[1], ny - d[1])

    chips = []
    for d in sorted(((a, b) for a in range(nz) for b in range(ny) if a or b), key=lambda d: (hops(d), d)):
        opposite = ((nz - d[0]) % nz, (ny - d[1]) % ny)
        for e in (d, opposite):
            if e not in chips:
                chips.append(e)
    return [(0, 0, 0), (0, 0, 1)] + [(a, b, c) for c in (0, 1) for n, (a, b) in enumerate(chips)]


def kernel(
    n_lon, n_lat, own_h,
    st, bg, kd, rad, w1h, w2h, w3h, cwh,
    acc,
    s0, s1, kap, rst, cols, send_r, send_c, recv_r, recv_c, rep_s, rep_0, rep_1,
    w1, w2, w3, cw, bgv, frc_a, frc_b, rim_s, rim_r, flux, edge_s, edge_r, own, pick, slotk, place,
    a1, g1, a2, g2, mis, gg2, gg1,
    load_sem, cs_sem, cr_sem, rs_sem, rr_sem, ps_sem, pr_sem,
    ns_s, ns_r, ew_s, ew_r,
):
    rows, fields, width, levels = st.shape
    halves = width // BLK
    nz, ny = torus(n_lon)
    order = offset_order(n_lon)
    chunk = min(CHUNK, n_lon // 4)
    chunks = n_lon // chunk
    lon = lax.axis_index("lon")
    lat = lax.axis_index("lat")
    core = lax.rem(lon, 2)
    yy = lax.rem(lon // 2, ny)
    zz = lon // (2 * ny)
    z_at = [lax.rem(zz + d, nz) * (2 * ny) for d in range(nz)]
    y_at = [lax.rem(yy + d, ny) * 2 for d in range(ny)]
    c_at = [core, 1 - core]

    rep_r = (rep_0, rep_1)

    def to(k):
        a, b, c = order[k]
        return (z_at[a] + y_at[b] + c_at[c], lat)

    def back(k):
        a, b, c = order[k]
        return (z_at[(nz - a) % nz] + y_at[(ny - b) % ny] + c_at[c], lat)

    up = (lon, lax.rem(lat + 1, n_lat))
    down = (lon, lax.rem(lat + n_lat - 1, n_lat))
    east = (lax.rem(lon + 1, n_lon), lat)
    west = (lax.rem(lon + n_lon - 1, n_lon), lat)
    inner = pl.ds(PAD, width)

    loads = [
        (st, s0.at[pl.ds(1, rows), :, inner, :]), (rad.at[1], rst.at[1]), (kd, kap.at[pl.ds(1, rows)]),
        (rad.at[0], rst.at[0]), (own_h, own), (w1h, w1), (w2h, w2), (w3h, w3), (cwh, cw), (bg, bgv),
    ]
    loads = [pltpu.make_async_copy(src, dst, load_sem.at[i]) for i, (src, dst) in enumerate(loads)]
    for load in loads[:5]:
        load.start()

    barrier = pltpu.get_barrier_semaphore()
    for k in range(1, n_lon):
        pl.semaphore_signal(barrier, inc=1, device_id=to(k), device_id_type=MESH)
    for there in (up, down):
        pl.semaphore_signal(barrier, inc=1, device_id=there, device_id_type=MESH)
    for load in loads[5:]:
        load.start()

    for k, (a, b, c) in enumerate(order):
        place[(a * ny + b) * 2 + c] = k

    def find_blocks(slot):
        found = []
        for b in range(own.shape[2]):
            owner = own[slot, 0, b]
            a = lax.rem(owner // (2 * ny) - zz + nz, nz)
            d = lax.rem(lax.rem(owner // 2, ny) - yy + ny, ny)
            c = lax.rem(lax.rem(owner, 2) + core, 2)
            found.append(place[(a * ny + d) * 2 + c])
            slotk[slot, b] = found[-1]

        @pl.loop(0, n_lon)
        def _(k):
            block = jnp.int32(0)
            for b, at in enumerate(found):
                block = jnp.where(at == k, b, block)
            pick[slot, k] = block

    def remote(src, dst, send_sem, recv_sem, there):
        return pltpu.make_async_remote_copy(
            src_ref=src, dst_ref=dst, send_sem=send_sem, recv_sem=recv_sem,
            device_id=there, device_id_type=MESH,
        )

    def send_rows(phase, row_up, to_up, row_down, to_down):
        remote(row_up, to_up, ns_s.at[phase, 0], ns_r.at[phase, 0], up).start()
        remote(row_down, to_down, ns_s.at[phase, 1], ns_r.at[phase, 1], down).start()

    def send_edges(phase):
        for side, there in ((0, east), (1, west)):
            remote(
                edge_s.at[phase, side], edge_r.at[phase, side],
                ew_s.at[phase, side], ew_r.at[phase, side], there,
            ).start()

    def wait_rows(phase, row_up, to_up, row_down, to_down):
        remote(row_up, to_up, ns_s.at[phase, 0], ns_r.at[phase, 0], up).wait()
        remote(row_down, to_down, ns_s.at[phase, 1], ns_r.at[phase, 1], down).wait()

    def wait_edges(phase):
        for side, there in ((0, east), (1, west)):
            remote(
                edge_s.at[phase, side], edge_r.at[phase, side],
                ew_s.at[phase, side], ew_r.at[phase, side], there,
            ).wait()

    def state_rows(s):
        return (
            s.at[rows, :, inner, :], s.at[0, :, inner, :],
            s.at[1, :, inner, :], s.at[rows + 1, :, inner, :],
        )

    def pack_state(phase, s):
        @pl.loop(0, rows)
        def _(i):
            for f in range(fields):
                edge_s[phase, 0, i, f : f + 1, :] = s[i + 1, f, PAD + width - 1 : PAD + width, :]
                edge_s[phase, 1, i, f : f + 1, :] = s[i + 1, f, PAD : PAD + 1, :]

    def send_state(phase, s):
        send_rows(phase, *state_rows(s))
        send_edges(phase)

    def take_state(phase, s):
        wait_rows(phase, *state_rows(s))
        wait_edges(phase)

        @pl.loop(0, rows)
        def _(i):
            for f in range(fields):
                s[i + 1, f, PAD - 1 : PAD, :] = edge_r[phase, 0, i, f : f + 1, :]
                s[i + 1, f, PAD + width : PAD + width + 1, :] = edge_r[phase, 1, i, f : f + 1, :]

        @pl.when(lat == 0)
        def _():
            s[0, :, PAD : PAD + width, :] = jnp.zeros((fields, width, levels), F32)

        @pl.when(lat == n_lat - 1)
        def _():
            s[rows + 1, :, PAD : PAD + width, :] = jnp.zeros((fields, width, levels), F32)

    level = lax.broadcasted_iota(jnp.int32, (BLK, levels), 1)
    from_below = jnp.where(level == 0, 0.0, VERTICAL).astype(F32)
    from_above = jnp.where(level == levels - 1, 0.0, VERTICAL).astype(F32)

    def vertical(v):
        return from_below * pltpu.roll(v, 1, 1) + from_above * pltpu.roll(v, levels - 1, 1)

    def advance(s, slot, keep):
        @pl.loop(0, rows)
        def _(i):
            for h in range(halves):
                at = PAD + h * BLK
                k = kap[i + 1, h * BLK : (h + 1) * BLK, :]
                u = ADVECT * s[i + 1, 0, at : at + BLK, :]
                v = ADVECT * s[i + 1, 1, at : at + BLK, :]
                k_e, k_w, k_n, k_s = k - u, k + u, k - v, k + v
                k_c = (1.0 - 2.0 * VERTICAL) - 4.0 * k
                for f in range(fields):
                    c = s[i + 1, f, at : at + BLK, :]
                    new = (
                        k_c * c
                        + k_e * s[i + 1, f, at + 1 : at + 1 + BLK, :]
                        + k_w * s[i + 1, f, at - 1 : at - 1 + BLK, :]
                        + k_n * s[i + 2, f, at : at + BLK, :]
                        + k_s * s[i, f, at : at + BLK, :]
                        + vertical(c)
                    )
                    if keep is not None:
                        keep[i + 1, f, at : at + BLK, :] = new
                    cols[slot, i * halves + h, :, f * levels : (f + 1) * levels] = new.astype(BF16)

    def pack(slot, blocks, sent, got):
        got[slot, 0] = blocks[slot, pick[slot, 0]]
        for k in range(1, n_lon):
            sent[slot, k] = blocks[slot, pick[slot, k]]

    def dispatch(slot, sent, got, send_sem, recv_sem):
        for k in range(1, n_lon):
            remote(
                sent.at[slot, k], got.at[slot, k], send_sem.at[slot],
                recv_sem.at[slot, k // chunk], to(k),
            ).start()

    def send_columns(slot):
        recv_c[slot, 0] = cols[slot, pick[slot, 0]]
        for k in range(1, n_lon):
            send_c[slot, k] = cols[slot, pick[slot, k]]
            remote(
                send_c.at[slot, k], recv_c.at[slot, k], cs_sem.at[slot],
                cr_sem.at[slot, k // chunk], to(k),
            ).start()

    loads[4].wait()
    find_blocks(1)
    loads[0].wait()
    pack_state(0, s0)
    loads[1].wait()
    loads[3].wait()
    pack(1, rst, send_r, recv_r)
    pl.semaphore_wait(barrier, n_lon + 1)
    send_state(0, s0)
    dispatch(1, send_r, recv_r, rs_sem, rr_sem)
    find_blocks(0)
    pack(0, rst, send_r, recv_r)
    loads[2].wait()
    take_state(0, s0)
    advance(s0, 0, s1)
    pack_state(1, s1)
    send_state(1, s1)
    dispatch(0, send_r, recv_r, rs_sem, rr_sem)
    take_state(1, s1)
    advance(s1, 1, None)
    send_columns(1)
    send_columns(0)
    for load in loads[5:]:
        load.wait()

    @pl.loop(0, rows)
    def _(i):
        for f in range(fields):
            bgv[i, f] = s0[i + 1, f, PAD : PAD + width, :] - bgv[i, f]

    for i in (0, rows + 1):
        kap[i] = jnp.zeros((width, levels), F32)
        frc_a[i] = jnp.zeros((fields, width, levels), F32)
        frc_b[i] = jnp.zeros((fields, width, levels), F32)

    span = chunk * BLK
    h1, h2, ch, cin = w1.shape[1], w2.shape[1], w3.shape[1], w1.shape[0]

    def tiles(n):
        return [slice(a, min(a + TILE, n)) for a in range(0, n, TILE)]

    def nn(a, b):
        return lax.dot_general(a, b, (((1,), (0,)), ((), ())), preferred_element_type=F32)

    def nt(a, b):
        return lax.dot_general(a, b, (((1,), (1,)), ((), ())), preferred_element_type=F32)

    def activate(z):
        sig = 0.5 * jnp.tanh(0.5 * z) + 0.5
        act = z * sig
        return act.astype(BF16), sig + act * (1.0 - sig)

    def wait_chunk(got, sem, slot, g):
        for first in (True, False):
            @pl.when((g == 0) if first else (g > 0))
            def _():
                part = got.at[slot, pl.ds(1, chunk - 1)] if first else got.at[slot, pl.ds(g * chunk, chunk)]
                pltpu.make_async_copy(part, part, sem.at[slot, g]).wait()

    @pl.loop(0, 2 * chunks)
    def _(t):
        slot = 1 - t // chunks
        g = lax.rem(t, chunks)
        base = g * chunk
        wait_chunk(recv_r, rr_sem, slot, g)
        wait_chunk(recv_c, cr_sem, slot, g)
        for n in tiles(h1):
            x = recv_c[slot, pl.ds(base, chunk)].reshape(span, cin)
            a1[:, n], g1[:, n] = activate(nn(x, w1[:, n]))
        for n in tiles(h2):
            a2[:, n], g2[:, n] = activate(nn(a1[...], w2[:, n]))
        for n in tiles(ch):
            y = recv_r[slot, pl.ds(base, chunk), :, n].reshape(span, n.stop - n.start).astype(F32)
            mis[:, n] = (cw[:, n] * (nn(a2[...], w3[:, n]) - y)).astype(BF16)
        for n in tiles(h2):
            gg2[:, n] = (nt(mis[...], w3[n, :]) * g2[:, n]).astype(BF16)
        for n in tiles(h1):
            gg1[:, n] = (nt(gg2[...], w2[n, :]) * g1[:, n]).astype(BF16)
        for n in tiles(cin):
            rep_s[slot, pl.ds(base, chunk), :, n] = (
                nt(gg1[...], w1[n, :]).astype(BF16).reshape(chunk, BLK, n.stop - n.start)
            )
        for tt in range(2 * chunks):
            @pl.when(t == tt)
            def _():
                home, replies = 1 - tt // chunks, rep_r[1 - tt // chunks]
                for k in range(tt % chunks * chunk, (tt % chunks + 1) * chunk):
                    if k == 0:
                        replies[0] = rep_s[home, 0]
                    else:
                        remote(
                            rep_s.at[home, k], replies.at[k], ps_sem.at[home],
                            pr_sem.at[home], back(k),
                        ).start()


    def wait_replies(slot):
        part = rep_r[slot].at[pl.ds(1, n_lon - 1)]
        pltpu.make_async_copy(part, part, pr_sem.at[slot]).wait()

    def forced(slot, i, h, f):
        return rep_r[slot][slotk[slot, i * halves + h], :, f * levels : (f + 1) * levels].astype(F32)

    def rims(phase):
        out_rim, in_rim = rim_s.at[phase - 2], rim_r.at[phase - 2]
        return (out_rim.at[0], in_rim.at[0], out_rim.at[1], in_rim.at[1])

    def send_rims(phase, s, g):
        for side, i, sign in ((0, rows, -1.0), (1, 1, 1.0)):
            for h in range(halves):
                part = slice(h * BLK, (h + 1) * BLK)
                coef = kap[i, part, :] + (sign * ADVECT) * s[i, 1, PAD + h * BLK : PAD + (h + 1) * BLK, :]
                for f in range(fields):
                    rim_s[phase - 2, side, f, part, :] = (coef * g[i, f, part, :]).astype(BF16)
        send_rows(phase, *rims(phase))

    def send_sides(phase, s, g):
        @pl.loop(0, rows)
        def _(i):
            for side, j, sign in ((0, width - 1, -1.0), (1, 0, 1.0)):
                coef = kap[i + 1, j : j + 1, :] + (sign * ADVECT) * s[i + 1, 0, PAD + j : PAD + j + 1, :]
                for f in range(fields):
                    edge_s[phase, side, i, f : f + 1, :] = coef * g[i + 1, f, j : j + 1, :]

        send_edges(phase)

    for f in range(fields):
        flux[0, f, 0:PAD, :] = jnp.zeros((PAD, levels), F32)
        flux[1, f, PAD + width :, :] = jnp.zeros((PAD, levels), F32)

    def transpose_tile(s, g, into, shift, extra):
        @pl.loop(0, rows)
        def _(i):
            for h in range(halves):
                at = PAD + h * BLK
                k = kap[i + 1, h * BLK : (h + 1) * BLK, :]
                u = ADVECT * s[i + 1, 0, at : at + BLK, :]
                k_e, k_w = k - u, k + u
                for f in range(fields):
                    own_g = g[i + 1, f, h * BLK : (h + 1) * BLK, :]
                    flux[0, f, at : at + BLK, :] = k_e * own_g
                    flux[1, f, at : at + BLK, :] = k_w * own_g
            for h in range(halves):
                part = slice(h * BLK, (h + 1) * BLK)
                at = PAD + h * BLK
                k_c = (1.0 - 2.0 * VERTICAL) - 4.0 * kap[i + 1, part, :]
                k_n = kap[i, part, :] - ADVECT * s[i, 1, at : at + BLK, :]
                k_s = kap[i + 2, part, :] + ADVECT * s[i + 2, 1, at : at + BLK, :]
                zonal = jnp.zeros((BLK, levels), F32)
                merid = jnp.zeros((BLK, levels), F32)
                for f in reversed(range(fields)):
                    own_g = g[i + 1, f, part, :]
                    zonal += own_g * (
                        s[i + 1, f, at + 1 : at + 1 + BLK, :] - s[i + 1, f, at - 1 : at - 1 + BLK, :]
                    )
                    merid += own_g * (s[i + 2, f, at : at + BLK, :] - s[i, f, at : at + BLK, :])
                    total = (
                        k_c * own_g + vertical(own_g)
                        + k_n * g[i, f, part, :] + k_s * g[i + 2, f, part, :]
                        + flux[0, f, at - 1 : at - 1 + BLK, :] + flux[1, f, at + 1 : at + 1 + BLK, :]
                    )
                    if extra is not None:
                        total += extra[i, f, part, :]
                    if f == 0:
                        total -= ADVECT * zonal
                    into[i + shift, f, part, :] = total
                into[i + shift, 1, part, :] -= ADVECT * merid

    def add_sides(phase, into, shift):
        wait_edges(phase)

        @pl.loop(0, rows)
        def _(i):
            for f in range(fields):
                into[i + shift, f, 0:1, :] += edge_r[phase, 0, i, f : f + 1, :]
                into[i + shift, f, width - 1 : width, :] += edge_r[phase, 1, i, f : f + 1, :]

    def add_rims(phase, into, shift):
        wait_rows(phase, *rims(phase))
        for side, i, there in ((0, 0, lat > 0), (1, rows - 1, lat < n_lat - 1)):
            @pl.when(there)
            def _():
                for f in range(fields):
                    into[i + shift, f] += rim_r[phase - 2, side, f].astype(F32)

    def add_forced(i):
        for h in range(halves):
            for f in range(fields):
                frc_b[i + 1, f, h * BLK : (h + 1) * BLK, :] += forced(0, i, h, f)

    wait_replies(1)

    @pl.loop(0, rows)
    def _(i):
        for h in range(halves):
            for f in range(fields):
                frc_a[i + 1, f, h * BLK : (h + 1) * BLK, :] = forced(1, i, h, f)

    send_rims(2, s1, frc_a)
    send_sides(2, s1, frc_a)
    transpose_tile(s1, frc_a, frc_b, 1, None)
    add_sides(2, frc_b, 1)
    add_rims(2, frc_b, 1)

    wait_replies(0)
    add_forced(0)
    add_forced(rows - 1)
    send_rims(3, s0, frc_b)
    pl.loop(1, rows - 1)(add_forced)
    send_sides(3, s0, frc_b)
    transpose_tile(s0, frc_b, acc, 0, bgv)
    add_sides(3, acc, 0)
    add_rims(3, acc, 0)

    for slot in (0, 1):
        for buffer, sem in ((send_r, rs_sem), (send_c, cs_sem), (rep_s, ps_sem)):
            part = buffer.at[slot, pl.ds(1, n_lon - 1)]
            pltpu.make_async_copy(part, part, sem.at[slot]).wait()


def shards(state, background, diffusivity, radiances, owners, first, second, third, weight):
    n_lon, n_lat = lax.axis_size("lon"), lax.axis_size("lat")
    rows, width, fields, levels = state.shape
    blocks = owners.shape[2]
    channels = radiances.shape[3]
    cin, h1, h2 = first.shape[1], first.shape[2], second.shape[2]
    chunk = min(CHUNK, n_lon // 4)
    span = chunk * BLK

    hbm = pl.BlockSpec(memory_space=pltpu.HBM)
    dma = pltpu.SemaphoreType.DMA
    body = functools.partial(kernel, n_lon, n_lat)
    slots = 2
    field = (rows, fields, width, levels)
    result = pl.pallas_call(
        body,
        out_shape=pltpu.VMEM(field, F32),
        in_specs=[hbm] * 9,
        out_specs=pl.BlockSpec(memory_space=pltpu.VMEM),
        scratch_shapes=[
            pltpu.VMEM((rows + 2, fields, width + 2 * PAD, levels), F32),
            pltpu.VMEM((rows + 2, fields, width + 2 * PAD, levels), F32),
            pltpu.VMEM((rows + 2, width, levels), F32),
            pltpu.VMEM((slots, blocks, BLK, channels), BF16),
            pltpu.VMEM((slots, blocks, BLK, cin), BF16),
            pltpu.VMEM((slots, n_lon, BLK, channels), BF16),
            pltpu.VMEM((slots, n_lon, BLK, cin), BF16),
            pltpu.VMEM((slots, n_lon, BLK, channels), BF16),
            pltpu.VMEM((slots, n_lon, BLK, cin), BF16),
            pltpu.VMEM((slots, n_lon, BLK, cin), BF16),
            pltpu.VMEM((n_lon, BLK, cin), BF16),
            pltpu.VMEM((n_lon, BLK, cin), BF16),
            pltpu.VMEM((cin, h1), BF16),
            pltpu.VMEM((h1, h2), BF16),
            pltpu.VMEM((h2, channels), BF16),
            pltpu.VMEM((1, channels), F32),
            pltpu.VMEM(field, F32),
            pltpu.VMEM((rows + 2, fields, width, levels), F32),
            pltpu.VMEM((rows + 2, fields, width, levels), F32),
            pltpu.VMEM((2, 2, fields, width, levels), BF16),
            pltpu.VMEM((2, 2, fields, width, levels), BF16),
            pltpu.VMEM((2, fields, width + 2 * PAD, levels), F32),
            pltpu.VMEM((4, 2, rows, 8, levels), F32),
            pltpu.VMEM((4, 2, rows, 8, levels), F32),
            pltpu.SMEM((slots, 1, blocks), jnp.int32),
            pltpu.SMEM((slots, n_lon), jnp.int32),
            pltpu.SMEM((slots, blocks), jnp.int32),
            pltpu.SMEM((n_lon,), jnp.int32),
            pltpu.VMEM((span, h1), BF16),
            pltpu.VMEM((span, h1), F32),
            pltpu.VMEM((span, h2), BF16),
            pltpu.VMEM((span, h2), F32),
            pltpu.VMEM((span, channels), BF16),
            pltpu.VMEM((span, h2), BF16),
            pltpu.VMEM((span, h1), BF16),
            dma((10,)),
            dma((slots,)),
            dma((slots, n_lon // chunk)),
            dma((slots,)),
            dma((slots, n_lon // chunk)),
            dma((slots,)),
            dma((slots,)),
            dma((4, 2)),
            dma((4, 2)),
            dma((4, 2)),
            dma((4, 2)),
        ],
        compiler_params=pltpu.CompilerParams(
            collective_id=0, has_side_effects=True, vmem_limit_bytes=60 * 2**20
        ),
        name="gradient",
    )(
        owners,
        state.transpose(0, 2, 1, 3),
        background.transpose(0, 2, 1, 3),
        diffusivity,
        radiances.reshape(slots, blocks, BLK, channels),
        first[0],
        second[0],
        third[0],
        weight,
    )
    return result.transpose(0, 2, 1, 3)


def solution(mesh):
    placed = (
        P("lat", "lon", None, None),
        P("lat", "lon", None, None),
        P("lat", "lon", None),
        P(None, "lat", "lon", None),
        P(None, "lat", "lon"),
        P("lon", None, None),
        P("lon", None, None),
        P("lon", None, None),
        P("lon", None),
    )
    return jax.shard_map(
        shards, mesh=mesh, in_specs=placed, out_specs=P("lat", "lon", None, None), check_vma=False
    )
```

```python
import functools

import jax
import jax.numpy as jnp
from jax import lax
from jax.experimental import pallas as pl
from jax.experimental.pallas import tpu as pltpu
from jax.sharding import PartitionSpec as P

MESH = pl.DeviceIdType.MESH
F32 = jnp.float32
BF16 = jnp.bfloat16
ADVECT = 0.125
VERTICAL = 0.1
BLK = 32
CHUNK = 8
HELD = 2
TILE = 256
PAD = 8


def torus(n_lon):
    chips = n_lon // 2
    ny = 1
    while ny * ny < chips:
        ny *= 2
    return chips // ny, ny


def offset_order(n_lon):
    nz, ny = torus(n_lon)

    def hops(d):
        return min(d[0], nz - d[0]) + min(d[1], ny - d[1])

    chips = []
    for d in sorted(((a, b) for a in range(nz) for b in range(ny) if a or b), key=lambda d: (0 in d and hops(d) > 1, hops(d), -d[0])):
        opposite = ((nz - d[0]) % nz, (ny - d[1]) % ny)
        for e in (d, opposite):
            if e not in chips:
                chips.append(e)
    return [(0, 0, 0), (0, 0, 1)] + [(a, b, c) for c in (0, 1) for n, (a, b) in enumerate(chips)]


def kernel(
    n_lon, n_lat, own_h,
    st, bg, kd, rad, w1h, w2h, w3h, cwh,
    acc,
    s0, s1, kap, rst, cols, send_r, send_c, recv_r, recv_c, rep_s, rep_0, rep_1,
    w1, w2, w3, cw, bgv, frc_a, frc_b, rim_s, rim_r, flux, edge_s, edge_r, own, pick, slotk, place,
    a1, g1, a2, g2, mis, gg2, gg1,
    load_sem, cs_sem, cr_sem, rs_sem, rr_sem, ps_sem, pr_sem,
    ns_s, ns_r, ew_s, ew_r,
):
    rows, fields, width, levels = st.shape
    halves = width // BLK
    nz, ny = torus(n_lon)
    order = offset_order(n_lon)
    chunk = min(CHUNK, n_lon // 4)
    chunks = n_lon // chunk
    lon = lax.axis_index("lon")
    lat = lax.axis_index("lat")
    core = lax.rem(lon, 2)
    yy = lax.rem(lon // 2, ny)
    zz = lon // (2 * ny)
    z_at = [lax.rem(zz + d, nz) * (2 * ny) for d in range(nz)]
    y_at = [lax.rem(yy + d, ny) * 2 for d in range(ny)]
    c_at = [core, 1 - core]

    rep_r = (rep_0, rep_1)

    def to(k):
        a, b, c = order[k]
        return (z_at[a] + y_at[b] + c_at[c], lat)

    def back(k):
        a, b, c = order[k]
        return (z_at[(nz - a) % nz] + y_at[(ny - b) % ny] + c_at[c], lat)

    up = (lon, lax.rem(lat + 1, n_lat))
    down = (lon, lax.rem(lat + n_lat - 1, n_lat))
    east = (lax.rem(lon + 1, n_lon), lat)
    west = (lax.rem(lon + n_lon - 1, n_lon), lat)
    inner = pl.ds(PAD, width)

    loads = [
        (st, s0.at[pl.ds(1, rows), :, inner, :]), (rad.at[1], rst.at[1]), (kd, kap.at[pl.ds(1, rows)]),
        (rad.at[0], rst.at[0]), (own_h, own), (w1h, w1), (w2h, w2), (w3h, w3), (cwh, cw), (bg, bgv),
    ]
    loads = [pltpu.make_async_copy(src, dst, load_sem.at[i]) for i, (src, dst) in enumerate(loads)]
    for load in loads[:5]:
        load.start()

    barrier = pltpu.get_barrier_semaphore()
    for k in range(1, n_lon):
        pl.semaphore_signal(barrier, inc=1, device_id=to(k), device_id_type=MESH)
    for there in (up, down):
        pl.semaphore_signal(barrier, inc=1, device_id=there, device_id_type=MESH)
    for load in loads[5:]:
        load.start()

    for k, (a, b, c) in enumerate(order):
        place[(a * ny + b) * 2 + c] = k

    def find_blocks(slot):
        found = []
        for b in range(own.shape[2]):
            owner = own[slot, 0, b]
            a = lax.rem(owner // (2 * ny) - zz + nz, nz)
            d = lax.rem(lax.rem(owner // 2, ny) - yy + ny, ny)
            c = lax.rem(lax.rem(owner, 2) + core, 2)
            found.append(place[(a * ny + d) * 2 + c])
            slotk[slot, b] = found[-1]

        @pl.loop(0, n_lon)
        def _(k):
            block = jnp.int32(0)
            for b, at in enumerate(found):
                block = jnp.where(at == k, b, block)
            pick[slot, k] = block

    def remote(src, dst, send_sem, recv_sem, there):
        return pltpu.make_async_remote_copy(
            src_ref=src, dst_ref=dst, send_sem=send_sem, recv_sem=recv_sem,
            device_id=there, device_id_type=MESH,
        )

    def send_rows(phase, row_up, to_up, row_down, to_down):
        remote(row_up, to_up, ns_s.at[phase, 0], ns_r.at[phase, 0], up).start()
        remote(row_down, to_down, ns_s.at[phase, 1], ns_r.at[phase, 1], down).start()

    def send_edges(phase):
        for side, there in ((0, east), (1, west)):
            remote(
                edge_s.at[phase, side], edge_r.at[phase, side],
                ew_s.at[phase, side], ew_r.at[phase, side], there,
            ).start()

    def wait_rows(phase, row_up, to_up, row_down, to_down):
        remote(row_up, to_up, ns_s.at[phase, 0], ns_r.at[phase, 0], up).wait()
        remote(row_down, to_down, ns_s.at[phase, 1], ns_r.at[phase, 1], down).wait()

    def wait_edges(phase):
        for side, there in ((0, east), (1, west)):
            remote(
                edge_s.at[phase, side], edge_r.at[phase, side],
                ew_s.at[phase, side], ew_r.at[phase, side], there,
            ).wait()

    def state_rows(s):
        return (
            s.at[rows, :, inner, :], s.at[0, :, inner, :],
            s.at[1, :, inner, :], s.at[rows + 1, :, inner, :],
        )

    def pack_state(phase, s):
        @pl.loop(0, rows)
        def _(i):
            for f in range(fields):
                edge_s[phase, 0, i, f : f + 1, :] = s[i + 1, f, PAD + width - 1 : PAD + width, :]
                edge_s[phase, 1, i, f : f + 1, :] = s[i + 1, f, PAD : PAD + 1, :]

    def send_state(phase, s):
        send_rows(phase, *state_rows(s))
        send_edges(phase)

    def take_state(phase, s):
        wait_rows(phase, *state_rows(s))
        wait_edges(phase)

        @pl.loop(0, rows)
        def _(i):
            for f in range(fields):
                s[i + 1, f, PAD - 1 : PAD, :] = edge_r[phase, 0, i, f : f + 1, :]
                s[i + 1, f, PAD + width : PAD + width + 1, :] = edge_r[phase, 1, i, f : f + 1, :]

        @pl.when(lat == 0)
        def _():
            s[0, :, PAD : PAD + width, :] = jnp.zeros((fields, width, levels), F32)

        @pl.when(lat == n_lat - 1)
        def _():
            s[rows + 1, :, PAD : PAD + width, :] = jnp.zeros((fields, width, levels), F32)

    level = lax.broadcasted_iota(jnp.int32, (BLK, levels), 1)
    from_below = jnp.where(level == 0, 0.0, VERTICAL).astype(F32)
    from_above = jnp.where(level == levels - 1, 0.0, VERTICAL).astype(F32)

    def vertical(v):
        return from_below * pltpu.roll(v, 1, 1) + from_above * pltpu.roll(v, levels - 1, 1)

    def advance(s, slot, keep):
        @pl.loop(0, rows)
        def _(i):
            for h in range(halves):
                at = PAD + h * BLK
                k = kap[i + 1, h * BLK : (h + 1) * BLK, :]
                u = ADVECT * s[i + 1, 0, at : at + BLK, :]
                v = ADVECT * s[i + 1, 1, at : at + BLK, :]
                k_e, k_w, k_n, k_s = k - u, k + u, k - v, k + v
                k_c = (1.0 - 2.0 * VERTICAL) - 4.0 * k
                for f in range(fields):
                    c = s[i + 1, f, at : at + BLK, :]
                    new = (
                        k_c * c
                        + k_e * s[i + 1, f, at + 1 : at + 1 + BLK, :]
                        + k_w * s[i + 1, f, at - 1 : at - 1 + BLK, :]
                        + k_n * s[i + 2, f, at : at + BLK, :]
                        + k_s * s[i, f, at : at + BLK, :]
                        + vertical(c)
                    )
                    if keep is not None:
                        keep[i + 1, f, at : at + BLK, :] = new
                    cols[slot, i * halves + h, :, f * levels : (f + 1) * levels] = new.astype(BF16)

    def pack(slot, blocks, sent, got):
        got[slot, 0] = blocks[slot, pick[slot, 0]]
        for k in range(1, n_lon):
            sent[slot, k] = blocks[slot, pick[slot, k]]

    def dispatch(slot, sent, got, send_sem, recv_sem):
        for k in range(1, n_lon):
            remote(
                sent.at[slot, k], got.at[slot, k], send_sem.at[slot],
                recv_sem.at[slot, k // chunk], to(k),
            ).start()

    def send_columns(slot):
        recv_c[slot, 0] = cols[slot, pick[slot, 0]]
        for k in range(1, n_lon):
            send_c[slot, k] = cols[slot, pick[slot, k]]
            remote(
                send_c.at[slot, k], recv_c.at[slot, k], cs_sem.at[slot],
                cr_sem.at[slot, k // chunk], to(k),
            ).start()

    loads[4].wait()
    find_blocks(1)
    loads[0].wait()
    pack_state(0, s0)
    loads[1].wait()
    loads[3].wait()
    pack(1, rst, send_r, recv_r)
    pl.semaphore_wait(barrier, n_lon + 1)
    send_state(0, s0)
    dispatch(1, send_r, recv_r, rs_sem, rr_sem)
    find_blocks(0)
    pack(0, rst, send_r, recv_r)
    loads[2].wait()
    take_state(0, s0)
    advance(s0, 0, s1)
    pack_state(1, s1)
    send_state(1, s1)
    dispatch(0, send_r, recv_r, rs_sem, rr_sem)
    take_state(1, s1)
    advance(s1, 1, None)
    send_columns(1)
    send_columns(0)
    for load in loads[5:]:
        load.wait()

    @pl.loop(0, rows)
    def _(i):
        for f in range(fields):
            bgv[i, f] = s0[i + 1, f, PAD : PAD + width, :] - bgv[i, f]

    for i in (0, rows + 1):
        kap[i] = jnp.zeros((width, levels), F32)
        frc_a[i] = jnp.zeros((fields, width, levels), F32)
        frc_b[i] = jnp.zeros((fields, width, levels), F32)

    span = chunk * BLK
    h1, h2, ch, cin = w1.shape[1], w2.shape[1], w3.shape[1], w1.shape[0]

    def tiles(n):
        return [slice(a, min(a + TILE, n)) for a in range(0, n, TILE)]

    def nn(a, b):
        return lax.dot_general(a, b, (((1,), (0,)), ((), ())), preferred_element_type=F32)

    def nt(a, b):
        return lax.dot_general(a, b, (((1,), (1,)), ((), ())), preferred_element_type=F32)

    def activate(z):
        sig = 0.5 * jnp.tanh(0.5 * z) + 0.5
        act = z * sig
        return act.astype(BF16), sig + act * (1.0 - sig)

    def wait_chunk(got, sem, slot, g):
        for first in (True, False):
            @pl.when((g == 0) if first else (g > 0))
            def _():
                part = got.at[slot, pl.ds(1, chunk - 1)] if first else got.at[slot, pl.ds(g * chunk, chunk)]
                pltpu.make_async_copy(part, part, sem.at[slot, g]).wait()

    def reply(home, g):
        replies = rep_r[home]
        for k in range(g * chunk, (g + 1) * chunk):
            if k == 0:
                replies[0] = rep_s[home, 0]
            else:
                remote(
                    rep_s.at[home, k], replies.at[k], ps_sem.at[home], pr_sem.at[home], back(k)
                ).start()

    @pl.loop(0, 2 * chunks)
    def _(t):
        slot = 1 - t // chunks
        g = lax.rem(t, chunks)
        base = g * chunk
        wait_chunk(recv_r, rr_sem, slot, g)
        wait_chunk(recv_c, cr_sem, slot, g)
        for n in tiles(h1):
            x = recv_c[slot, pl.ds(base, chunk)].reshape(span, cin)
            a1[:, n], g1[:, n] = activate(nn(x, w1[:, n]))
        for n in tiles(h2):
            a2[:, n], g2[:, n] = activate(nn(a1[...], w2[:, n]))
        for n in tiles(ch):
            y = recv_r[slot, pl.ds(base, chunk), :, n].reshape(span, n.stop - n.start).astype(F32)
            mis[:, n] = (cw[:, n] * (nn(a2[...], w3[:, n]) - y)).astype(BF16)
        for n in tiles(h2):
            gg2[:, n] = (nt(mis[...], w3[n, :]) * g2[:, n]).astype(BF16)
        for n in tiles(h1):
            gg1[:, n] = (nt(gg2[...], w2[n, :]) * g1[:, n]).astype(BF16)
        for n in tiles(cin):
            rep_s[slot, pl.ds(base, chunk), :, n] = (
                nt(gg1[...], w1[n, :]).astype(BF16).reshape(chunk, BLK, n.stop - n.start)
            )
        for tt in range(2 * chunks - HELD):
            @pl.when(t == tt)
            def _():
                reply(1 - tt // chunks, tt % chunks)


    def wait_replies(slot):
        part = rep_r[slot].at[pl.ds(1, n_lon - 1)]
        pltpu.make_async_copy(part, part, pr_sem.at[slot]).wait()

    def forced(slot, i, h, f):
        return rep_r[slot][slotk[slot, i * halves + h], :, f * levels : (f + 1) * levels].astype(F32)

    def rims(phase):
        out_rim, in_rim = rim_s.at[phase - 2], rim_r.at[phase - 2]
        return (out_rim.at[0], in_rim.at[0], out_rim.at[1], in_rim.at[1])

    def send_rims(phase, s, g):
        for side, i, sign in ((0, rows, -1.0), (1, 1, 1.0)):
            for h in range(halves):
                part = slice(h * BLK, (h + 1) * BLK)
                coef = kap[i, part, :] + (sign * ADVECT) * s[i, 1, PAD + h * BLK : PAD + (h + 1) * BLK, :]
                for f in range(fields):
                    rim_s[phase - 2, side, f, part, :] = (coef * g[i, f, part, :]).astype(BF16)
        send_rows(phase, *rims(phase))

    def send_sides(phase, s, g):
        @pl.loop(0, rows)
        def _(i):
            for side, j, sign in ((0, width - 1, -1.0), (1, 0, 1.0)):
                coef = kap[i + 1, j : j + 1, :] + (sign * ADVECT) * s[i + 1, 0, PAD + j : PAD + j + 1, :]
                for f in range(fields):
                    edge_s[phase, side, i, f : f + 1, :] = coef * g[i + 1, f, j : j + 1, :]

        send_edges(phase)

    for f in range(fields):
        flux[0, f, 0:PAD, :] = jnp.zeros((PAD, levels), F32)
        flux[1, f, PAD + width :, :] = jnp.zeros((PAD, levels), F32)

    def transpose_tile(s, g, into, shift, extra):
        @pl.loop(0, rows)
        def _(i):
            for h in range(halves):
                at = PAD + h * BLK
                k = kap[i + 1, h * BLK : (h + 1) * BLK, :]
                u = ADVECT * s[i + 1, 0, at : at + BLK, :]
                k_e, k_w = k - u, k + u
                for f in range(fields):
                    own_g = g[i + 1, f, h * BLK : (h + 1) * BLK, :]
                    flux[0, f, at : at + BLK, :] = k_e * own_g
                    flux[1, f, at : at + BLK, :] = k_w * own_g
            for h in range(halves):
                part = slice(h * BLK, (h + 1) * BLK)
                at = PAD + h * BLK
                k_c = (1.0 - 2.0 * VERTICAL) - 4.0 * kap[i + 1, part, :]
                k_n = kap[i, part, :] - ADVECT * s[i, 1, at : at + BLK, :]
                k_s = kap[i + 2, part, :] + ADVECT * s[i + 2, 1, at : at + BLK, :]
                zonal = jnp.zeros((BLK, levels), F32)
                merid = jnp.zeros((BLK, levels), F32)
                for f in reversed(range(fields)):
                    own_g = g[i + 1, f, part, :]
                    zonal += own_g * (
                        s[i + 1, f, at + 1 : at + 1 + BLK, :] - s[i + 1, f, at - 1 : at - 1 + BLK, :]
                    )
                    merid += own_g * (s[i + 2, f, at : at + BLK, :] - s[i, f, at : at + BLK, :])
                    total = (
                        k_c * own_g + vertical(own_g)
                        + k_n * g[i, f, part, :] + k_s * g[i + 2, f, part, :]
                        + flux[0, f, at - 1 : at - 1 + BLK, :] + flux[1, f, at + 1 : at + 1 + BLK, :]
                    )
                    if extra is not None:
                        total += extra[i, f, part, :]
                    if f == 0:
                        total -= ADVECT * zonal
                    into[i + shift, f, part, :] = total
                into[i + shift, 1, part, :] -= ADVECT * merid

    def add_sides(phase, into, shift):
        wait_edges(phase)

        @pl.loop(0, rows)
        def _(i):
            for f in range(fields):
                into[i + shift, f, 0:1, :] += edge_r[phase, 0, i, f : f + 1, :]
                into[i + shift, f, width - 1 : width, :] += edge_r[phase, 1, i, f : f + 1, :]

    def add_rims(phase, into, shift):
        wait_rows(phase, *rims(phase))
        for side, i, there in ((0, 0, lat > 0), (1, rows - 1, lat < n_lat - 1)):
            @pl.when(there)
            def _():
                for f in range(fields):
                    into[i + shift, f] += rim_r[phase - 2, side, f].astype(F32)

    def add_forced(i):
        for h in range(halves):
            for f in range(fields):
                frc_b[i + 1, f, h * BLK : (h + 1) * BLK, :] += forced(0, i, h, f)

    wait_replies(1)

    @pl.loop(0, rows)
    def _(i):
        for h in range(halves):
            for f in range(fields):
                frc_a[i + 1, f, h * BLK : (h + 1) * BLK, :] = forced(1, i, h, f)

    send_rims(2, s1, frc_a)
    send_sides(2, s1, frc_a)
    for g in range(chunks - HELD, chunks):
        reply(0, g)
    transpose_tile(s1, frc_a, frc_b, 1, None)
    add_sides(2, frc_b, 1)
    add_rims(2, frc_b, 1)

    wait_replies(0)
    add_forced(0)
    add_forced(rows - 1)
    send_rims(3, s0, frc_b)
    pl.loop(1, rows - 1)(add_forced)
    send_sides(3, s0, frc_b)
    transpose_tile(s0, frc_b, acc, 0, bgv)
    add_sides(3, acc, 0)
    add_rims(3, acc, 0)

    for slot in (0, 1):
        for buffer, sem in ((send_r, rs_sem), (send_c, cs_sem), (rep_s, ps_sem)):
            part = buffer.at[slot, pl.ds(1, n_lon - 1)]
            pltpu.make_async_copy(part, part, sem.at[slot]).wait()


def shards(state, background, diffusivity, radiances, owners, first, second, third, weight):
    n_lon, n_lat = lax.axis_size("lon"), lax.axis_size("lat")
    rows, width, fields, levels = state.shape
    blocks = owners.shape[2]
    channels = radiances.shape[3]
    cin, h1, h2 = first.shape[1], first.shape[2], second.shape[2]
    chunk = min(CHUNK, n_lon // 4)
    span = chunk * BLK

    hbm = pl.BlockSpec(memory_space=pltpu.HBM)
    dma = pltpu.SemaphoreType.DMA
    body = functools.partial(kernel, n_lon, n_lat)
    slots = 2
    field = (rows, fields, width, levels)
    result = pl.pallas_call(
        body,
        out_shape=pltpu.VMEM(field, F32),
        in_specs=[hbm] * 9,
        out_specs=pl.BlockSpec(memory_space=pltpu.VMEM),
        scratch_shapes=[
            pltpu.VMEM((rows + 2, fields, width + 2 * PAD, levels), F32),
            pltpu.VMEM((rows + 2, fields, width + 2 * PAD, levels), F32),
            pltpu.VMEM((rows + 2, width, levels), F32),
            pltpu.VMEM((slots, blocks, BLK, channels), BF16),
            pltpu.VMEM((slots, blocks, BLK, cin), BF16),
            pltpu.VMEM((slots, n_lon, BLK, channels), BF16),
            pltpu.VMEM((slots, n_lon, BLK, cin), BF16),
            pltpu.VMEM((slots, n_lon, BLK, channels), BF16),
            pltpu.VMEM((slots, n_lon, BLK, cin), BF16),
            pltpu.VMEM((slots, n_lon, BLK, cin), BF16),
            pltpu.VMEM((n_lon, BLK, cin), BF16),
            pltpu.VMEM((n_lon, BLK, cin), BF16),
            pltpu.VMEM((cin, h1), BF16),
            pltpu.VMEM((h1, h2), BF16),
            pltpu.VMEM((h2, channels), BF16),
            pltpu.VMEM((1, channels), F32),
            pltpu.VMEM(field, F32),
            pltpu.VMEM((rows + 2, fields, width, levels), F32),
            pltpu.VMEM((rows + 2, fields, width, levels), F32),
            pltpu.VMEM((2, 2, fields, width, levels), BF16),
            pltpu.VMEM((2, 2, fields, width, levels), BF16),
            pltpu.VMEM((2, fields, width + 2 * PAD, levels), F32),
            pltpu.VMEM((4, 2, rows, 8, levels), F32),
            pltpu.VMEM((4, 2, rows, 8, levels), F32),
            pltpu.SMEM((slots, 1, blocks), jnp.int32),
            pltpu.SMEM((slots, n_lon), jnp.int32),
            pltpu.SMEM((slots, blocks), jnp.int32),
            pltpu.SMEM((n_lon,), jnp.int32),
            pltpu.VMEM((span, h1), BF16),
            pltpu.VMEM((span, h1), F32),
            pltpu.VMEM((span, h2), BF16),
            pltpu.VMEM((span, h2), F32),
            pltpu.VMEM((span, channels), BF16),
            pltpu.VMEM((span, h2), BF16),
            pltpu.VMEM((span, h1), BF16),
            dma((10,)),
            dma((slots,)),
            dma((slots, n_lon // chunk)),
            dma((slots,)),
            dma((slots, n_lon // chunk)),
            dma((slots,)),
            dma((slots,)),
            dma((4, 2)),
            dma((4, 2)),
            dma((4, 2)),
            dma((4, 2)),
        ],
        compiler_params=pltpu.CompilerParams(
            collective_id=0, has_side_effects=True, vmem_limit_bytes=60 * 2**20
        ),
        name="gradient",
    )(
        owners,
        state.transpose(0, 2, 1, 3),
        background.transpose(0, 2, 1, 3),
        diffusivity,
        radiances.reshape(slots, blocks, BLK, channels),
        first[0],
        second[0],
        third[0],
        weight,
    )
    return result.transpose(0, 2, 1, 3)


def solution(mesh):
    placed = (
        P("lat", "lon", None, None),
        P("lat", "lon", None, None),
        P("lat", "lon", None),
        P(None, "lat", "lon", None),
        P(None, "lat", "lon"),
        P("lon", None, None),
        P("lon", None, None),
        P("lon", None, None),
        P("lon", None),
    )
    return jax.shard_map(
        shards, mesh=mesh, in_specs=placed, out_specs=P("lat", "lon", None, None), check_vma=False
    )
```

```python
import functools

import jax
import jax.numpy as jnp
from jax import lax
from jax.experimental import pallas as pl
from jax.experimental.pallas import tpu as pltpu
from jax.sharding import PartitionSpec as P

MESH = pl.DeviceIdType.MESH
F32 = jnp.float32
BF16 = jnp.bfloat16
ADVECT = 0.125
VERTICAL = 0.1
BLK = 32
CHUNK = 8
HELD = 2
TILE = 256
PAD = 8


def torus(n_lon):
    chips = n_lon // 2
    ny = 1
    while ny * ny < chips:
        ny *= 2
    return chips // ny, ny


def offset_order(n_lon):
    nz, ny = torus(n_lon)

    def hops(d):
        return min(d[0], nz - d[0]) + min(d[1], ny - d[1])

    chips = []
    for d in sorted(((a, b) for a in range(nz) for b in range(ny) if a or b), key=lambda d: (0 in d and hops(d) > 1, hops(d), -d[0])):
        opposite = ((nz - d[0]) % nz, (ny - d[1]) % ny)
        for e in (d, opposite):
            if e not in chips:
                chips.append(e)
    return [(0, 0, 0), (0, 0, 1)] + [(a, b, c) for c in (0, 1) for n, (a, b) in enumerate(chips)]


def kernel(
    n_lon, n_lat, own_h,
    st, bg, kd, rad, w1h, w2h, w3h, cwh,
    acc,
    s0, s1, kap, rst, cols, send_r, send_c, recv_r, recv_c, rep_s, rep_0, rep_1,
    w1, w2, w3, cw, bgv, frc_a, frc_b, rim_s, rim_r, flux, edge_s, edge_r, own, pick, slotk, place,
    a1, g1, a2, g2, mis, gg2, gg1,
    load_sem, cs_sem, cr_sem, rs_sem, rr_sem, ps_sem, pr_sem,
    ns_s, ns_r, ew_s, ew_r,
):
    rows, fields, width, levels = st.shape
    halves = width // BLK
    nz, ny = torus(n_lon)
    order = offset_order(n_lon)
    chunk = min(CHUNK, n_lon // 4)
    chunks = n_lon // chunk
    lon = lax.axis_index("lon")
    lat = lax.axis_index("lat")
    core = lax.rem(lon, 2)
    yy = lax.rem(lon // 2, ny)
    zz = lon // (2 * ny)
    z_at = [lax.rem(zz + d, nz) * (2 * ny) for d in range(nz)]
    y_at = [lax.rem(yy + d, ny) * 2 for d in range(ny)]
    c_at = [core, 1 - core]

    rep_r = (rep_0, rep_1)

    def to(k):
        a, b, c = order[k]
        return (z_at[a] + y_at[b] + c_at[c], lat)

    def back(k):
        a, b, c = order[k]
        return (z_at[(nz - a) % nz] + y_at[(ny - b) % ny] + c_at[c], lat)

    up = (lon, lax.rem(lat + 1, n_lat))
    down = (lon, lax.rem(lat + n_lat - 1, n_lat))
    east = (lax.rem(lon + 1, n_lon), lat)
    west = (lax.rem(lon + n_lon - 1, n_lon), lat)
    inner = pl.ds(PAD, width)

    loads = [
        (st, s0.at[pl.ds(1, rows), :, inner, :]), (rad.at[1], rst.at[1]), (kd, kap.at[pl.ds(1, rows)]),
        (rad.at[0], rst.at[0]), (own_h, own), (w1h, w1), (w2h, w2), (w3h, w3), (cwh, cw), (bg, bgv),
    ]
    loads = [pltpu.make_async_copy(src, dst, load_sem.at[i]) for i, (src, dst) in enumerate(loads)]
    for load in loads[:5]:
        load.start()

    barrier = pltpu.get_barrier_semaphore()
    for k in range(1, n_lon):
        pl.semaphore_signal(barrier, inc=1, device_id=to(k), device_id_type=MESH)
    for there in (up, down):
        pl.semaphore_signal(barrier, inc=1, device_id=there, device_id_type=MESH)
    for load in loads[5:]:
        load.start()

    for k, (a, b, c) in enumerate(order):
        place[(a * ny + b) * 2 + c] = k

    def find_blocks(slot):
        found = []
        for b in range(own.shape[2]):
            owner = own[slot, 0, b]
            a = lax.rem(owner // (2 * ny) - zz + nz, nz)
            d = lax.rem(lax.rem(owner // 2, ny) - yy + ny, ny)
            c = lax.rem(lax.rem(owner, 2) + core, 2)
            found.append(place[(a * ny + d) * 2 + c])
            slotk[slot, b] = found[-1]

        @pl.loop(0, n_lon)
        def _(k):
            block = jnp.int32(0)
            for b, at in enumerate(found):
                block = jnp.where(at == k, b, block)
            pick[slot, k] = block

    def remote(src, dst, send_sem, recv_sem, there):
        return pltpu.make_async_remote_copy(
            src_ref=src, dst_ref=dst, send_sem=send_sem, recv_sem=recv_sem,
            device_id=there, device_id_type=MESH,
        )

    def send_rows(phase, row_up, to_up, row_down, to_down):
        remote(row_up, to_up, ns_s.at[phase, 0], ns_r.at[phase, 0], up).start()
        remote(row_down, to_down, ns_s.at[phase, 1], ns_r.at[phase, 1], down).start()

    def send_edges(phase):
        for side, there in ((0, east), (1, west)):
            remote(
                edge_s.at[phase, side], edge_r.at[phase, side],
                ew_s.at[phase, side], ew_r.at[phase, side], there,
            ).start()

    def wait_rows(phase, row_up, to_up, row_down, to_down):
        remote(row_up, to_up, ns_s.at[phase, 0], ns_r.at[phase, 0], up).wait()
        remote(row_down, to_down, ns_s.at[phase, 1], ns_r.at[phase, 1], down).wait()

    def wait_edges(phase):
        for side, there in ((0, east), (1, west)):
            remote(
                edge_s.at[phase, side], edge_r.at[phase, side],
                ew_s.at[phase, side], ew_r.at[phase, side], there,
            ).wait()

    def state_rows(s):
        return (
            s.at[rows, :, inner, :], s.at[0, :, inner, :],
            s.at[1, :, inner, :], s.at[rows + 1, :, inner, :],
        )

    def pack_state(phase, s):
        @pl.loop(0, rows, unroll=True)
        def _(i):
            for f in range(fields):
                edge_s[phase, 0, i, f : f + 1, :] = s[i + 1, f, PAD + width - 1 : PAD + width, :]
                edge_s[phase, 1, i, f : f + 1, :] = s[i + 1, f, PAD : PAD + 1, :]

    def send_state(phase, s):
        send_rows(phase, *state_rows(s))
        send_edges(phase)

    def take_state(phase, s):
        wait_rows(phase, *state_rows(s))
        wait_edges(phase)

        @pl.loop(0, rows, unroll=True)
        def _(i):
            for f in range(fields):
                s[i + 1, f, PAD - 1 : PAD, :] = edge_r[phase, 0, i, f : f + 1, :]
                s[i + 1, f, PAD + width : PAD + width + 1, :] = edge_r[phase, 1, i, f : f + 1, :]

        @pl.when(lat == 0)
        def _():
            s[0, :, PAD : PAD + width, :] = jnp.zeros((fields, width, levels), F32)

        @pl.when(lat == n_lat - 1)
        def _():
            s[rows + 1, :, PAD : PAD + width, :] = jnp.zeros((fields, width, levels), F32)

    level = lax.broadcasted_iota(jnp.int32, (BLK, levels), 1)
    from_below = jnp.where(level == 0, 0.0, VERTICAL).astype(F32)
    from_above = jnp.where(level == levels - 1, 0.0, VERTICAL).astype(F32)

    def vertical(v):
        return from_below * pltpu.roll(v, 1, 1) + from_above * pltpu.roll(v, levels - 1, 1)

    def advance(s, slot, keep):
        @pl.loop(0, rows)
        def _(i):
            for h in range(halves):
                at = PAD + h * BLK
                k = kap[i + 1, h * BLK : (h + 1) * BLK, :]
                u = ADVECT * s[i + 1, 0, at : at + BLK, :]
                v = ADVECT * s[i + 1, 1, at : at + BLK, :]
                k_e, k_w, k_n, k_s = k - u, k + u, k - v, k + v
                k_c = (1.0 - 2.0 * VERTICAL) - 4.0 * k
                for f in range(fields):
                    c = s[i + 1, f, at : at + BLK, :]
                    new = (
                        k_c * c
                        + k_e * s[i + 1, f, at + 1 : at + 1 + BLK, :]
                        + k_w * s[i + 1, f, at - 1 : at - 1 + BLK, :]
                        + k_n * s[i + 2, f, at : at + BLK, :]
                        + k_s * s[i, f, at : at + BLK, :]
                        + vertical(c)
                    )
                    if keep is not None:
                        keep[i + 1, f, at : at + BLK, :] = new
                    cols[slot, i * halves + h, :, f * levels : (f + 1) * levels] = new.astype(BF16)

    def pack(slot, blocks, sent, got):
        got[slot, 0] = blocks[slot, pick[slot, 0]]
        for k in range(1, n_lon):
            sent[slot, k] = blocks[slot, pick[slot, k]]

    def dispatch(slot, sent, got, send_sem, recv_sem):
        for k in range(1, n_lon):
            remote(
                sent.at[slot, k], got.at[slot, k], send_sem.at[slot],
                recv_sem.at[slot, k // chunk], to(k),
            ).start()

    def send_columns(slot):
        recv_c[slot, 0] = cols[slot, pick[slot, 0]]
        for k in range(1, n_lon):
            send_c[slot, k] = cols[slot, pick[slot, k]]
            remote(
                send_c.at[slot, k], recv_c.at[slot, k], cs_sem.at[slot],
                cr_sem.at[slot, k // chunk], to(k),
            ).start()

    loads[4].wait()
    find_blocks(1)
    loads[0].wait()
    pack_state(0, s0)
    loads[1].wait()
    loads[3].wait()
    pack(1, rst, send_r, recv_r)
    pl.semaphore_wait(barrier, n_lon + 1)
    send_state(0, s0)
    dispatch(1, send_r, recv_r, rs_sem, rr_sem)
    find_blocks(0)
    pack(0, rst, send_r, recv_r)
    loads[2].wait()
    take_state(0, s0)
    advance(s0, 0, s1)
    pack_state(1, s1)
    send_state(1, s1)
    dispatch(0, send_r, recv_r, rs_sem, rr_sem)
    take_state(1, s1)
    advance(s1, 1, None)
    send_columns(1)
    send_columns(0)
    for load in loads[5:]:
        load.wait()

    @pl.loop(0, rows)
    def _(i):
        for f in range(fields):
            bgv[i, f] = s0[i + 1, f, PAD : PAD + width, :] - bgv[i, f]

    for i in (0, rows + 1):
        kap[i] = jnp.zeros((width, levels), F32)
        frc_a[i] = jnp.zeros((fields, width, levels), F32)
        frc_b[i] = jnp.zeros((fields, width, levels), F32)

    span = chunk * BLK
    h1, h2, ch, cin = w1.shape[1], w2.shape[1], w3.shape[1], w1.shape[0]

    def tiles(n):
        return [slice(a, min(a + TILE, n)) for a in range(0, n, TILE)]

    def nn(a, b):
        return lax.dot_general(a, b, (((1,), (0,)), ((), ())), preferred_element_type=F32)

    def nt(a, b):
        return lax.dot_general(a, b, (((1,), (1,)), ((), ())), preferred_element_type=F32)

    def activate(z):
        sig = 0.5 * jnp.tanh(0.5 * z) + 0.5
        act = z * sig
        return act.astype(BF16), sig + act * (1.0 - sig)

    def wait_chunk(got, sem, slot, g):
        for first in (True, False):
            @pl.when((g == 0) if first else (g > 0))
            def _():
                part = got.at[slot, pl.ds(1, chunk - 1)] if first else got.at[slot, pl.ds(g * chunk, chunk)]
                pltpu.make_async_copy(part, part, sem.at[slot, g]).wait()

    def reply(home, g):
        replies = rep_r[home]
        for k in range(g * chunk, (g + 1) * chunk):
            if k == 0:
                replies[0] = rep_s[home, 0]
            else:
                remote(
                    rep_s.at[home, k], replies.at[k], ps_sem.at[home], pr_sem.at[home], back(k)
                ).start()

    @pl.loop(0, 2 * chunks)
    def _(t):
        slot = 1 - t // chunks
        g = lax.rem(t, chunks)
        base = g * chunk
        wait_chunk(recv_r, rr_sem, slot, g)
        wait_chunk(recv_c, cr_sem, slot, g)
        for n in tiles(h1):
            x = recv_c[slot, pl.ds(base, chunk)].reshape(span, cin)
            a1[:, n], g1[:, n] = activate(nn(x, w1[:, n]))
        for n in tiles(h2):
            a2[:, n], g2[:, n] = activate(nn(a1[...], w2[:, n]))
        for n in tiles(ch):
            y = recv_r[slot, pl.ds(base, chunk), :, n].reshape(span, n.stop - n.start).astype(F32)
            mis[:, n] = (cw[:, n] * (nn(a2[...], w3[:, n]) - y)).astype(BF16)
        for n in tiles(h2):
            gg2[:, n] = (nt(mis[...], w3[n, :]) * g2[:, n]).astype(BF16)
        for n in tiles(h1):
            gg1[:, n] = (nt(gg2[...], w2[n, :]) * g1[:, n]).astype(BF16)
        for n in tiles(cin):
            rep_s[slot, pl.ds(base, chunk), :, n] = (
                nt(gg1[...], w1[n, :]).astype(BF16).reshape(chunk, BLK, n.stop - n.start)
            )
        for tt in range(2 * chunks - HELD):
            @pl.when(t == tt)
            def _():
                reply(1 - tt // chunks, tt % chunks)


    def wait_replies(slot):
        part = rep_r[slot].at[pl.ds(1, n_lon - 1)]
        pltpu.make_async_copy(part, part, pr_sem.at[slot]).wait()

    def forced(slot, i, h, f):
        return rep_r[slot][slotk[slot, i * halves + h], :, f * levels : (f + 1) * levels].astype(F32)

    def rims(phase):
        out_rim, in_rim = rim_s.at[phase - 2], rim_r.at[phase - 2]
        return (out_rim.at[0], in_rim.at[0], out_rim.at[1], in_rim.at[1])

    def send_rims(phase, s, g):
        for side, i, sign in ((0, rows, -1.0), (1, 1, 1.0)):
            for h in range(halves):
                part = slice(h * BLK, (h + 1) * BLK)
                coef = kap[i, part, :] + (sign * ADVECT) * s[i, 1, PAD + h * BLK : PAD + (h + 1) * BLK, :]
                for f in range(fields):
                    rim_s[phase - 2, side, f, part, :] = (coef * g[i, f, part, :]).astype(BF16)
        send_rows(phase, *rims(phase))

    def send_sides(phase, s, g):
        @pl.loop(0, rows, unroll=True)
        def _(i):
            for side, j, sign in ((0, width - 1, -1.0), (1, 0, 1.0)):
                coef = kap[i + 1, j : j + 1, :] + (sign * ADVECT) * s[i + 1, 0, PAD + j : PAD + j + 1, :]
                for f in range(fields):
                    edge_s[phase, side, i, f : f + 1, :] = coef * g[i + 1, f, j : j + 1, :]

        send_edges(phase)

    for f in range(fields):
        flux[0, f, 0:PAD, :] = jnp.zeros((PAD, levels), F32)
        flux[1, f, PAD + width :, :] = jnp.zeros((PAD, levels), F32)

    def transpose_tile(s, g, into, shift, extra):
        @pl.loop(0, rows)
        def _(i):
            for h in range(halves):
                at = PAD + h * BLK
                k = kap[i + 1, h * BLK : (h + 1) * BLK, :]
                u = ADVECT * s[i + 1, 0, at : at + BLK, :]
                k_e, k_w = k - u, k + u
                for f in range(fields):
                    own_g = g[i + 1, f, h * BLK : (h + 1) * BLK, :]
                    flux[0, f, at : at + BLK, :] = k_e * own_g
                    flux[1, f, at : at + BLK, :] = k_w * own_g
            for h in range(halves):
                part = slice(h * BLK, (h + 1) * BLK)
                at = PAD + h * BLK
                k_c = (1.0 - 2.0 * VERTICAL) - 4.0 * kap[i + 1, part, :]
                k_n = kap[i, part, :] - ADVECT * s[i, 1, at : at + BLK, :]
                k_s = kap[i + 2, part, :] + ADVECT * s[i + 2, 1, at : at + BLK, :]
                zonal = jnp.zeros((BLK, levels), F32)
                merid = jnp.zeros((BLK, levels), F32)
                for f in reversed(range(fields)):
                    own_g = g[i + 1, f, part, :]
                    zonal += own_g * (
                        s[i + 1, f, at + 1 : at + 1 + BLK, :] - s[i + 1, f, at - 1 : at - 1 + BLK, :]
                    )
                    merid += own_g * (s[i + 2, f, at : at + BLK, :] - s[i, f, at : at + BLK, :])
                    total = (
                        k_c * own_g + vertical(own_g)
                        + k_n * g[i, f, part, :] + k_s * g[i + 2, f, part, :]
                        + flux[0, f, at - 1 : at - 1 + BLK, :] + flux[1, f, at + 1 : at + 1 + BLK, :]
                    )
                    if extra is not None:
                        total += extra[i, f, part, :]
                    if f == 0:
                        total -= ADVECT * zonal
                    into[i + shift, f, part, :] = total
                into[i + shift, 1, part, :] -= ADVECT * merid

    def add_sides(phase, into, shift):
        wait_edges(phase)

        @pl.loop(0, rows, unroll=True)
        def _(i):
            for f in range(fields):
                into[i + shift, f, 0:1, :] += edge_r[phase, 0, i, f : f + 1, :]
                into[i + shift, f, width - 1 : width, :] += edge_r[phase, 1, i, f : f + 1, :]

    def add_rims(phase, into, shift):
        wait_rows(phase, *rims(phase))
        for side, i, there in ((0, 0, lat > 0), (1, rows - 1, lat < n_lat - 1)):
            @pl.when(there)
            def _():
                for f in range(fields):
                    into[i + shift, f] += rim_r[phase - 2, side, f].astype(F32)

    def add_forced(i):
        for h in range(halves):
            for f in range(fields):
                frc_b[i + 1, f, h * BLK : (h + 1) * BLK, :] += forced(0, i, h, f)

    wait_replies(1)

    @pl.loop(0, rows)
    def _(i):
        for h in range(halves):
            for f in range(fields):
                frc_a[i + 1, f, h * BLK : (h + 1) * BLK, :] = forced(1, i, h, f)

    send_rims(2, s1, frc_a)
    send_sides(2, s1, frc_a)
    for g in range(chunks - HELD, chunks):
        reply(0, g)
    transpose_tile(s1, frc_a, frc_b, 1, None)
    add_sides(2, frc_b, 1)
    add_rims(2, frc_b, 1)

    wait_replies(0)
    add_forced(0)
    add_forced(rows - 1)
    send_rims(3, s0, frc_b)
    pl.loop(1, rows - 1)(add_forced)
    send_sides(3, s0, frc_b)
    transpose_tile(s0, frc_b, acc, 0, bgv)
    add_sides(3, acc, 0)
    add_rims(3, acc, 0)

    for slot in (0, 1):
        for buffer, sem in ((send_r, rs_sem), (send_c, cs_sem), (rep_s, ps_sem)):
            part = buffer.at[slot, pl.ds(1, n_lon - 1)]
            pltpu.make_async_copy(part, part, sem.at[slot]).wait()


def shards(state, background, diffusivity, radiances, owners, first, second, third, weight):
    n_lon, n_lat = lax.axis_size("lon"), lax.axis_size("lat")
    rows, width, fields, levels = state.shape
    blocks = owners.shape[2]
    channels = radiances.shape[3]
    cin, h1, h2 = first.shape[1], first.shape[2], second.shape[2]
    chunk = min(CHUNK, n_lon // 4)
    span = chunk * BLK

    hbm = pl.BlockSpec(memory_space=pltpu.HBM)
    dma = pltpu.SemaphoreType.DMA
    body = functools.partial(kernel, n_lon, n_lat)
    slots = 2
    field = (rows, fields, width, levels)
    result = pl.pallas_call(
        body,
        out_shape=pltpu.VMEM(field, F32),
        in_specs=[hbm] * 9,
        out_specs=pl.BlockSpec(memory_space=pltpu.VMEM),
        scratch_shapes=[
            pltpu.VMEM((rows + 2, fields, width + 2 * PAD, levels), F32),
            pltpu.VMEM((rows + 2, fields, width + 2 * PAD, levels), F32),
            pltpu.VMEM((rows + 2, width, levels), F32),
            pltpu.VMEM((slots, blocks, BLK, channels), BF16),
            pltpu.VMEM((slots, blocks, BLK, cin), BF16),
            pltpu.VMEM((slots, n_lon, BLK, channels), BF16),
            pltpu.VMEM((slots, n_lon, BLK, cin), BF16),
            pltpu.VMEM((slots, n_lon, BLK, channels), BF16),
            pltpu.VMEM((slots, n_lon, BLK, cin), BF16),
            pltpu.VMEM((slots, n_lon, BLK, cin), BF16),
            pltpu.VMEM((n_lon, BLK, cin), BF16),
            pltpu.VMEM((n_lon, BLK, cin), BF16),
            pltpu.VMEM((cin, h1), BF16),
            pltpu.VMEM((h1, h2), BF16),
            pltpu.VMEM((h2, channels), BF16),
            pltpu.VMEM((1, channels), F32),
            pltpu.VMEM(field, F32),
            pltpu.VMEM((rows + 2, fields, width, levels), F32),
            pltpu.VMEM((rows + 2, fields, width, levels), F32),
            pltpu.VMEM((2, 2, fields, width, levels), BF16),
            pltpu.VMEM((2, 2, fields, width, levels), BF16),
            pltpu.VMEM((2, fields, width + 2 * PAD, levels), F32),
            pltpu.VMEM((4, 2, rows, 8, levels), F32),
            pltpu.VMEM((4, 2, rows, 8, levels), F32),
            pltpu.SMEM((slots, 1, blocks), jnp.int32),
            pltpu.SMEM((slots, n_lon), jnp.int32),
            pltpu.SMEM((slots, blocks), jnp.int32),
            pltpu.SMEM((n_lon,), jnp.int32),
            pltpu.VMEM((span, h1), BF16),
            pltpu.VMEM((span, h1), F32),
            pltpu.VMEM((span, h2), BF16),
            pltpu.VMEM((span, h2), F32),
            pltpu.VMEM((span, channels), BF16),
            pltpu.VMEM((span, h2), BF16),
            pltpu.VMEM((span, h1), BF16),
            dma((10,)),
            dma((slots,)),
            dma((slots, n_lon // chunk)),
            dma((slots,)),
            dma((slots, n_lon // chunk)),
            dma((slots,)),
            dma((slots,)),
            dma((4, 2)),
            dma((4, 2)),
            dma((4, 2)),
            dma((4, 2)),
        ],
        compiler_params=pltpu.CompilerParams(
            collective_id=0, has_side_effects=True, vmem_limit_bytes=60 * 2**20
        ),
        name="gradient",
    )(
        owners,
        state.transpose(0, 2, 1, 3),
        background.transpose(0, 2, 1, 3),
        diffusivity,
        radiances.reshape(slots, blocks, BLK, channels),
        first[0],
        second[0],
        third[0],
        weight,
    )
    return result.transpose(0, 2, 1, 3)


def solution(mesh):
    placed = (
        P("lat", "lon", None, None),
        P("lat", "lon", None, None),
        P("lat", "lon", None),
        P(None, "lat", "lon", None),
        P(None, "lat", "lon"),
        P("lon", None, None),
        P("lon", None, None),
        P("lon", None, None),
        P("lon", None),
    )
    return jax.shard_map(
        shards, mesh=mesh, in_specs=placed, out_specs=P("lat", "lon", None, None), check_vma=False
    )
```
